256 devices in a mesh: dp: 8 (over z), expert: 32 (over x, y, core).
Axes of the slice: x: 4, y: 4, z: 8, core: 2. Of those that a mesh axis runs over, the one named last changes fastest.
Arguments:
- tokens: bfloat16 [8192, 7168], P('expert', 'dp'), may hold values from -6 to 6
- out_grad: bfloat16 [8192, 7168], P('expert', 'dp'), may hold values from -6 to 6
- routes: int32 [8192, 2], P('expert'), may hold values from 0 to 31, all different within a row; in each aligned block of 256 rows (0 to 255, 256 to 511, ...) at most 32 rows name the same one
- route_weights: float32 [8192, 2], P('expert'), may hold values from 0.2 to 1
- w_gate: bfloat16 [32, 7168, 1024], P('expert', 'dp'), may hold values from -0.0625 to 0.0625
- w_up: bfloat16 [32, 7168, 1024], P('expert', 'dp'), may hold values from -0.0625 to 0.0625
- w_down: bfloat16 [32, 1024, 7168], P('expert', None, 'dp'), may hold values from -0.1875 to 0.1875
- p_in: bfloat16 [32, 2, 16, 7168], P('expert', None, None, 'dp'), may hold values from -0.0625 to 0.0625
- q_in: bfloat16 [32, 2, 16, 1024], P('expert'), may hold values from -0.75 to 0.75
- p_down: bfloat16 [32, 16, 1024], P('expert'), may hold values from -0.75 to 0.75
- q_down: bfloat16 [32, 16, 7168], P('expert', None, 'dp'), may hold values from -0.0625 to 0.0625
- lam: float32 [32, 3, 16], P('expert'), may hold values from 0.2 to 1
- rank_mask: int32 [32, 3, 16], P('expert'), may hold values 0 or 1
Outputs:
- input_grad: bfloat16 [8192, 7168], P('expert', 'dp')
- grad_q_in: float32 [32, 2, 16, 1024], P('expert', None, None, 'dp')
- grad_p_in: float32 [32, 2, 16, 7168], P('expert', None, None, 'dp')
- grad_p_down: float32 [32, 16, 1024], P('expert', None, 'dp')
- grad_q_down: float32 [32, 16, 7168], P('expert', None, 'dp')
- grad_lam: float32 [32, 3, 16], P('expert')
The draws below stay inside these ranges and needn't reach their ends.
Inputs may be any that keep to these rules, and one draw needn't show every extreme that they name: `routes`: each row names 2 different experts. In each aligned block of 256 rows no expert is named more than 32 times, a bound that some block reaches.
All inputs are finite; a program needn't handle non-finite values. No bound on the sum of `rank_mask` on one device may be relied on, other than what follows from the above.
Results may differ from the reference program's by a relative error of at most 0.03.
Values may be sent and summed in bfloat16 or wider, within the bound.
A program may use at most 128 MiB of HBM per device.

```python
import math
import jax
import jax.numpy as jnp
import numpy as np
from jax import lax

D = 7168
FF = 1024
RANK = 16
TOP = 2
TOK_DEV = 256
EXPERTS = 32
TOKENS = 8192
CAP = 32
N_DP = 8
N_EXPERT = 32


def touch_ends(entries, rng, smallest, largest):
    spot = [jax.random.randint(jax.random.fold_in(rng, axis), (), 0, length) for axis, length in enumerate(entries.shape)]
    widest = entries.shape.index(max(entries.shape))
    next_to = spot[:widest] + [(spot[widest] + 1) % entries.shape[widest]] + spot[widest + 1:]
    return entries.at[tuple(spot)].set(smallest).at[tuple(next_to)].set(largest)


def block_levels(stream_key, extent, shards, low, largest):
    def one(dim, shards_of):
        draws = jax.random.uniform(jax.random.fold_in(jax.random.fold_in(stream_key, 6), dim), (shards_of,), jnp.float32, low / len(shards), largest / len(shards))
        return jnp.repeat(jnp.exp(draws), extent[dim] // shards_of).reshape((-1,) + (1,) * (len(extent) - dim - 1))

    factor_of = one(*shards[0])
    for cut in shards[1:]:
        factor_of = factor_of * one(*cut)
    return factor_of


def assign_block(own_key, own, number, rows, amount, top, reach, skew):
    sequence = jax.random.permutation(own_key, amount)
    packed, common = portions_of(amount, rows * top, reach, skew, True), portions_of(amount, rows * top, reach, skew, False)
    places = jnp.arange(amount)

    def named(sizes, turn):
        used = int((sizes > 0).sum())
        fixed = max(1, used // 4)
        passed = fixed + (places - fixed + turn * (used - fixed)) % max(1, amount - fixed)
        return jnp.zeros((amount,), jnp.int32).at[sequence[jnp.where(places < fixed, places, passed)]].set(jnp.asarray(sizes, jnp.int32))

    sizes = jnp.where(number % 4 == 0, named(packed, number // 4), named(common, number - number // 4 - 1))
    mixed = jax.random.permutation(jax.random.fold_in(own, 3), amount)
    source_of, taker = mixed[0:amount // 2 * 2:2], mixed[1:amount // 2 * 2:2]
    margin = jnp.minimum(sizes[source_of] - 1, reach - sizes[taker]) // 2
    margin = jnp.where((source_of == sequence[0]) | (taker == sequence[0]) | (sizes[taker] == 0), 0, jnp.maximum(margin, 0))
    passed = jax.random.randint(jax.random.fold_in(own, 4), (amount // 2,), 0, 1 << 20) % (margin + 1)
    sizes = sizes.at[source_of].add(-passed).at[taker].add(passed)
    labels = jnp.searchsorted(jnp.cumsum(sizes), jnp.arange(rows * top), side="right").astype(jnp.int32)
    grid = labels.reshape(top, rows).T
    grid = grid[jax.random.permutation(jax.random.fold_in(own, 1), rows)]
    turn = jax.random.randint(jax.random.fold_in(own, 2), (rows, 1), 0, top)
    return jnp.take_along_axis(grid, (jnp.arange(top)[None, :] + turn) % top, axis=1)


def portions_of(number_of, total, limit, skew, full):
    weights = [(1 << 20) // math.isqrt(grade ** skew) + 1 for grade in range(1, number_of + 1)]
    largest = limit if full else min(limit, max(-(-total // number_of), total * weights[0] // sum(weights)))
    least = 1 if total - largest >= number_of - 1 else 0
    given, surplus = [largest] + [least] * (number_of - 1), total - largest - least * (number_of - 1)
    while surplus > 0:
        candidates = [i for i in range(1, number_of) if given[i] < largest] or [i for i in range(1, number_of) if given[i] < limit]
        whole, left = sum([weights[i] for i in candidates]), surplus
        for i in candidates:
            addition = min(limit - given[i], max(1, left * weights[i] // whole), surplus)
            given[i] = given[i] + addition
            surplus = surplus - addition
    return np.array(given)


def normal_values(own_key, shape, scale, bound, cuts=(), kind=jnp.bfloat16):
    drawn = scale * jax.random.normal(own_key, shape, jnp.float32)
    if cuts:
        drawn = drawn * block_levels(own_key, shape, cuts, -0.22, 0.18)
    return jnp.clip(drawn, -bound, bound).astype(kind)


def setup_inputs(seed: int = 0) -> dict:
    key_list = jax.random.split(jax.random.key(seed), 14)
    tokens = normal_values(key_list[0], (TOKENS, D), 1.0, 6.0, ((0, 32), (1, 8)))
    out_grad = normal_values(key_list[1], (TOKENS, D), 1.0, 6.0, ((0, 32), (1, 8)))
    routes_keys = jax.random.split(jax.random.fold_in(key_list[2], 1), TOKENS // TOK_DEV)
    routes_turns = jax.random.permutation(jax.random.fold_in(key_list[2], 3), TOKENS // TOK_DEV)
    routes = jax.vmap(lambda own, number: assign_block(jax.random.fold_in(key_list[2], 2), own, number, TOK_DEV, EXPERTS, TOP, CAP, 2))(routes_keys, routes_turns).reshape((TOKENS, TOP))
    route_weights = jnp.clip(0.2 + 0.8 * jax.random.uniform(key_list[3], (TOKENS, TOP), jnp.float32) ** block_levels(key_list[3], (TOKENS, TOP), ((0, 32),), -0.2, 0.2), 0.2, 1.0)
    w_gate = normal_values(key_list[4], (EXPERTS, D, FF), D ** -0.5, 0.0625, ((0, 32), (1, 8)))
    w_up = normal_values(key_list[5], (EXPERTS, D, FF), D ** -0.5, 0.0625, ((0, 32), (1, 8)))
    w_down = normal_values(key_list[6], (EXPERTS, FF, D), FF ** -0.5, 0.1875, ((0, 32), (2, 8)))
    p_in = normal_values(key_list[7], (EXPERTS, 2, RANK, D), D ** -0.5, 0.0625, ((0, 32), (3, 8)))
    q_in = normal_values(key_list[8], (EXPERTS, 2, RANK, FF), (4 * RANK) ** -0.5, 0.75, ((0, 32),))
    p_down = normal_values(key_list[9], (EXPERTS, RANK, FF), (4 * RANK) ** -0.5, 0.75, ((0, 32),))
    q_down = normal_values(key_list[10], (EXPERTS, RANK, D), D ** -0.5, 0.0625, ((0, 32), (2, 8)))
    lam = jnp.clip(0.2 + 0.8 * jax.random.uniform(key_list[11], (EXPERTS, 3, RANK), jnp.float32) ** block_levels(key_list[11], (EXPERTS, 3, RANK), ((0, 32),), -0.2, 0.2), 0.2, 1.0)
    rank_mask = touch_ends((jax.random.randint(key_list[12], (EXPERTS, 3, RANK), 0, 4) < 3).astype(jnp.int32), jax.random.fold_in(key_list[12], 1), 0, 1)
    return {"tokens": tokens, "out_grad": out_grad, "routes": routes, "route_weights": route_weights, "w_gate": w_gate, "w_up": w_up, "w_down": w_down, "p_in": p_in, "q_in": q_in, "p_down": p_down, "q_down": q_down, "lam": lam, "rank_mask": rank_mask}


HIGH_PRECISION = lax.Precision.HIGHEST


def silu_pair(values):
    sigmoid = 1.0 / (1.0 + jnp.exp(-values))
    return values * sigmoid, sigmoid * (1.0 + values * (1.0 - sigmoid))


def slot_numbers(expert_ids, expert_count):
    one_hot = (expert_ids[..., None] == jnp.arange(expert_count, dtype=jnp.int32)).astype(jnp.int32)
    before = jnp.cumsum(one_hot, axis=-2) - one_hot
    return jnp.sum(before * one_hot, axis=-1).astype(jnp.int32)


def contract_rows(left, right):
    return lax.dot_general(left, right, (((1,), (1,)), ((), ())), preferred_element_type=jnp.float32)


def contract_slots(left, right):
    return lax.dot_general(left, right, (((0,), (0,)), ((), ())), preferred_element_type=jnp.float32)


def rounded(values):
    return lax.optimization_barrier(values.astype(jnp.bfloat16)).astype(jnp.float32)


def finish_hidden(sums, ranks, gate_table, up_table, down_table, scale):
    gate_sum, up_sum, down_sum = sums
    rank_gate, rank_up, rank_grad = ranks
    gate_pre = gate_sum + jnp.dot(rank_gate * scale[0], gate_table.astype(jnp.float32), precision=HIGH_PRECISION)
    up_pre = up_sum + jnp.dot(rank_up * scale[1], up_table.astype(jnp.float32), precision=HIGH_PRECISION)
    hidden_grad = down_sum + jnp.dot(rank_grad * scale[2], down_table.astype(jnp.float32), precision=HIGH_PRECISION)
    activated, slope = silu_pair(gate_pre)
    hidden = (activated * up_pre).astype(jnp.bfloat16)
    gate_grad = (hidden_grad * up_pre * slope).astype(jnp.bfloat16)
    up_grad = (hidden_grad * activated).astype(jnp.bfloat16)
    return hidden, gate_grad, up_grad


def reference(tokens, out_grad, routes, route_weights, w_gate, w_up, w_down, p_in, q_in, p_down, q_down, lam, rank_mask):
    route_count = TOK_DEV * TOP
    block_ids = routes.reshape(N_EXPERT, route_count)
    slot_index = slot_numbers(block_ids, EXPERTS)
    sources = jnp.arange(N_EXPERT, dtype=jnp.int32)[:, None]
    route_ids = sources * route_count + jnp.arange(route_count, dtype=jnp.int32)[None, :]
    flat_weights = route_weights.reshape(-1)
    width = D // N_DP
    total_slots = N_EXPERT * CAP
    missing = TOKENS * TOP
    zero_half = jnp.zeros((), jnp.bfloat16)

    def per_expert(carry, expert):
        target = jnp.where(block_ids == expert, sources * CAP + slot_index, total_slots).astype(jnp.int32)
        table = jnp.full((total_slots,), missing, jnp.int32).at[target.reshape(-1)].set(route_ids.reshape(-1), mode="drop")
        live = table < missing
        route_pick = jnp.where(live, table, 0).astype(jnp.int32)
        token_pick = (route_pick // TOP).astype(jnp.int32)
        slot_tokens = jnp.where(live[:, None], tokens[token_pick], zero_half)
        scaled = (flat_weights[route_pick][:, None] * out_grad[token_pick].astype(jnp.float32)).astype(jnp.bfloat16)
        slot_grads = jnp.where(live[:, None], scaled, zero_half)
        gate_w = w_gate[expert]
        up_w = w_up[expert]
        down_w = w_down[expert]
        gate_left = p_in[expert, 0]
        up_left = p_in[expert, 1]
        down_right = q_down[expert]
        scale = lam[expert] * rank_mask[expert].astype(jnp.float32)
        gate_sum = jnp.zeros((total_slots, FF), jnp.float32)
        up_sum = jnp.zeros((total_slots, FF), jnp.float32)
        down_sum = jnp.zeros((total_slots, FF), jnp.float32)
        rank_gate = jnp.zeros((total_slots, RANK), jnp.float32)
        rank_up = jnp.zeros((total_slots, RANK), jnp.float32)
        rank_grad = jnp.zeros((total_slots, RANK), jnp.float32)
        for block_index in range(N_DP):
            low = block_index * width
            high = low + width
            part_tokens = slot_tokens[:, low:high]
            part_grads = slot_grads[:, low:high]
            gate_sum = gate_sum + rounded(jnp.dot(part_tokens, gate_w[low:high], preferred_element_type=jnp.float32))
            up_sum = up_sum + rounded(jnp.dot(part_tokens, up_w[low:high], preferred_element_type=jnp.float32))
            down_sum = down_sum + rounded(contract_rows(part_grads, down_w[:, low:high]))
            rank_gate = rank_gate + rounded(contract_rows(part_tokens, gate_left[:, low:high]))
            rank_up = rank_up + rounded(contract_rows(part_tokens, up_left[:, low:high]))
            rank_grad = rank_grad + rounded(contract_rows(part_grads, down_right[:, low:high]))
        hidden, gate_grad, up_grad = finish_hidden((gate_sum, up_sum, down_sum), (rank_gate, rank_up, rank_grad), q_in[expert, 0], q_in[expert, 1], p_down[expert], scale)
        gate_back = contract_rows(gate_grad, q_in[expert, 0])
        up_back = contract_rows(up_grad, q_in[expert, 1])
        gate_coef = (gate_back * scale[0]).astype(jnp.bfloat16)
        up_coef = (up_back * scale[1]).astype(jnp.bfloat16)
        route_input = contract_rows(gate_grad, gate_w) + contract_rows(up_grad, up_w)
        route_input = route_input + jnp.dot(gate_coef, gate_left, preferred_element_type=jnp.float32)
        route_input = route_input + jnp.dot(up_coef, up_left, preferred_element_type=jnp.float32)
        route_input = route_input.astype(jnp.bfloat16).astype(jnp.float32)
        carry = carry.at[token_pick].add(jnp.where(live[:, None], route_input, 0.0))
        gate_rank_scaled = (rank_gate * scale[0]).astype(jnp.bfloat16)
        up_rank_scaled = (rank_up * scale[1]).astype(jnp.bfloat16)
        grad_q = jnp.stack([contract_slots(gate_rank_scaled, gate_grad), contract_slots(up_rank_scaled, up_grad)])
        grad_p = jnp.stack([contract_slots(gate_coef, slot_tokens), contract_slots(up_coef, slot_tokens)])
        down_rank = contract_rows(hidden, p_down[expert])
        down_coef = (down_rank * scale[2]).astype(jnp.bfloat16)
        grad_coef = (rank_grad * scale[2]).astype(jnp.bfloat16)
        grad_pd = contract_slots(grad_coef, hidden)
        grad_qd = contract_slots(down_coef, slot_grads)
        grad_scale = jnp.stack([jnp.sum(rank_gate * gate_back, axis=0), jnp.sum(rank_up * up_back, axis=0), jnp.sum(down_rank * rank_grad, axis=0)])
        grad_scale = grad_scale * rank_mask[expert].astype(jnp.float32)
        return carry, (grad_q, grad_p, grad_pd, grad_qd, grad_scale)

    start = jnp.zeros((TOKENS, D), jnp.float32)
    total, outputs = lax.scan(per_expert, start, jnp.arange(EXPERTS, dtype=jnp.int32))
    return (total.astype(jnp.bfloat16), outputs[0], outputs[1], outputs[2], outputs[3], outputs[4])
```

```python
import functools

import jax
import jax.numpy as jnp
from jax import lax
from jax.experimental import pallas as pl
from jax.experimental.pallas import tpu as pltpu
from jax.sharding import PartitionSpec as P

MESH = pl.DeviceIdType.MESH
F32 = jnp.float32
BF16 = jnp.bfloat16
HIGH = lax.Precision.HIGHEST

D_BLOCK = 896
FF = 1024
RANK = 16
TOK = 256
CAP = 32
N_DP = 8
N_EXPERT = 32
CHUNKS = 4
SHARES = 8
ROWS = SHARES * CAP
W1 = 2 * FF
W2 = FF + 128
WA = 2 * FF + 128
CUT1 = 1024
CUT2 = 640
CUTA = 1024
OFFSETS = (
    ((0, 0), (1, 0), (3, 0), (0, 1)),
    ((2, 2), (2, 1), (2, 3), (1, 2)),
    ((3, 2), (2, 0), (0, 2), (3, 3)),
    ((0, 3), (1, 1), (3, 1), (1, 3)),
)


def dot_nn(a, b, precision=None):
    return lax.dot_general(a, b, (((1,), (0,)), ((), ())), precision=precision, preferred_element_type=F32)


def dot_nt(a, b, precision=None):
    return lax.dot_general(a, b, (((1,), (1,)), ((), ())), precision=precision, preferred_element_type=F32)


def dot_tn(a, b):
    return lax.dot_general(a, b, (((0,), (0,)), ((), ())), preferred_element_type=F32)


def pick(values, chunk):
    if isinstance(chunk, int):
        return values[chunk]
    out = values[0]
    for k in range(1, len(values)):
        out = jnp.where(chunk == k, values[k], out)
    return out


def kernel(
    routes_ref,
    weights_ref,
    tokens_hbm,
    grads_hbm,
    wg_hbm,
    wu_hbm,
    wd_hbm,
    p_in_ref,
    q_in_ref,
    p_down_ref,
    q_down_ref,
    lam_ref,
    mask_ref,
    in_grad_ref,
    gq_ref,
    gp_ref,
    gpd_ref,
    gqd_ref,
    gl_ref,
    tok,
    out_grad,
    wg,
    wu,
    wd,
    p_tok,
    p_grad,
    q_all,
    hot,
    send_t,
    send_g,
    recv_t,
    recv_g,
    part1,
    part2,
    ring1,
    ring2,
    gathered,
    route_out,
    returned,
    rank_part,
    hidden_own,
    acc_in,
    acc_pd,
    acc_lam,
    scale_row,
    pos,
    fin_send,
    fin_recv,
    load_sem,
    t_send,
    t_recv,
    g_send,
    g_recv,
    r_send,
    r_recv,
    rs1_send,
    rs1_recv,
    rs2_send,
    rs2_recv,
    ag_send,
    ag_recv,
    fin_ssem,
    fin_rsem,
):
    z = lax.axis_index("dp")
    e = lax.axis_index("expert")
    ex = e // 8
    ey = (e // 2) % 4
    ec = e % 2
    right = (z + 1) % N_DP
    left = (z + N_DP - 1) % N_DP

    def expert_at(chunk, j, sign):
        dx = pick([o[j // 2][0] for o in OFFSETS], chunk)
        dy = pick([o[j // 2][1] for o in OFFSETS], chunk)
        x = (ex + 4 + sign * dx) % 4
        y = (ey + 4 + sign * dy) % 4
        return (x * 4 + y) * 2 + (ec + j) % 2

    loads = []
    for k, (src, dst) in enumerate(
        (
            (tokens_hbm, tok),
            (grads_hbm, out_grad),
            (wg_hbm.at[0], wg),
            (wu_hbm.at[0], wu),
            (wd_hbm.at[0], wd),
        )
    ):
        copy = pltpu.make_async_copy(src, dst, load_sem.at[k])
        copy.start()
        loads.append(copy)

    barrier = pltpu.get_barrier_semaphore()
    for k in range(1, N_EXPERT):
        pl.semaphore_signal(barrier, inc=1, device_id=(z, (e + k) % N_EXPERT), device_id_type=MESH)
    for k in range(1, N_DP):
        pl.semaphore_signal(barrier, inc=1, device_id=((z + k) % N_DP, e), device_id_type=MESH)

    expert_iota = lax.broadcasted_iota(jnp.int32, (N_EXPERT, TOK), 0)
    named0 = (expert_iota == routes_ref[0:1, :]).astype(F32)
    named1 = (expert_iota == routes_ref[1:2, :]).astype(F32)
    earlier = (
        lax.broadcasted_iota(jnp.int32, (TOK, TOK), 0) < lax.broadcasted_iota(jnp.int32, (TOK, TOK), 1)
    ).astype(BF16)
    before = dot_nn((named0 + named1).astype(BF16), earlier)
    pos[0:1, :] = jnp.sum(named0 * before, axis=0, keepdims=True) + CAP * routes_ref[0:1, :].astype(F32)
    pos[1:2, :] = jnp.sum(named1 * before, axis=0, keepdims=True) + CAP * routes_ref[1:2, :].astype(F32)

    def route_sends(chunk, fn):
        for j in range(SHARES):
            fn(j)

    def t_copy(chunk, j):
        return pltpu.make_async_remote_copy(
            send_t.at[chunk, j], recv_t.at[chunk, j], t_send.at[chunk], t_recv.at[chunk],
            device_id=(z, expert_at(chunk, j, -1)), device_id_type=MESH,
        )

    def g_copy(chunk, j):
        return pltpu.make_async_remote_copy(
            send_g.at[chunk, j], recv_g.at[chunk, j], g_send.at[chunk], g_recv.at[chunk],
            device_id=(z, expert_at(chunk, j, -1)), device_id_type=MESH,
        )

    def r_copy(chunk, j):
        return pltpu.make_async_remote_copy(
            route_out.at[chunk, j], returned.at[chunk, j], r_send.at[chunk], r_recv.at[chunk],
            device_id=(z, expert_at(chunk, j, 1)), device_id_type=MESH,
        )

    def send_all(chunk, copy_of, src, dst, sem):
        for j in range(SHARES):
            if j == 0:
                @pl.when(chunk > 0)
                def _():
                    copy_of(chunk, 0).start()

                @pl.when(chunk == 0)
                def _():
                    pltpu.make_async_copy(src.at[chunk, 0], dst.at[chunk, 0], sem.at[chunk]).start()
            else:
                copy_of(chunk, j).start()

    def wait_chunk(ref, sem, chunk):
        pltpu.make_async_copy(ref.at[chunk], ref.at[chunk], sem.at[chunk]).wait()

    slot_iota = lax.broadcasted_iota(jnp.int32, (CAP, TOK), 0)

    def route_chunk(chunk):
        pos0, pos1 = pos[0:1, :], pos[1:2, :]
        weight0, weight1 = weights_ref[0:1, :], weights_ref[1:2, :]
        slot_weights = []
        for j in range(SHARES):
            target = (slot_iota + CAP * expert_at(chunk, j, -1)).astype(F32)
            hit0, hit1 = target == pos0, target == pos1
            hot[chunk, j * CAP:(j + 1) * CAP, :] = jnp.where(hit0 | hit1, 1.0, 0.0).astype(BF16)
            weight = jnp.where(hit0, weight0, 0.0) + jnp.where(hit1, weight1, 0.0)
            slot_weights.append(jnp.sum(weight, axis=1, keepdims=True))
        picked = dot_nn(hot[chunk], tok[...])
        send_t[chunk] = picked.astype(BF16).reshape(SHARES, CAP, D_BLOCK)
        send_all(chunk, t_copy, send_t, recv_t, t_recv)
        picked = dot_nn(hot[chunk], out_grad[...])
        for j in range(SHARES):
            send_g[chunk, j] = (slot_weights[j] * picked[j * CAP:(j + 1) * CAP, :]).astype(BF16)
        send_all(chunk, g_copy, send_g, recv_g, g_recv)

    def forward1(chunk):
        wait_chunk(recv_t, t_recv, chunk)

        @pl.loop(0, 4)
        def _(n):
            x = recv_t[chunk].reshape(ROWS, D_BLOCK)
            at = pl.ds(pl.multiple_of(n * 256, 256), 256)
            at_up = pl.ds(pl.multiple_of(n * 256 + FF, 256), 256)
            part1[chunk, :, :, at] = dot_nn(x, wg[:, at]).astype(BF16).reshape(SHARES, CAP, 256)
            part1[chunk, :, :, at_up] = dot_nn(x, wu[:, at]).astype(BF16).reshape(SHARES, CAP, 256)

    def forward2(chunk):
        rank_part[...] = dot_nt(recv_t[chunk].reshape(ROWS, D_BLOCK), p_tok[...])
        wait_chunk(recv_g, g_recv, chunk)
        y = recv_g[chunk].reshape(ROWS, D_BLOCK)
        ranks = rank_part[...] + dot_nt(y, p_grad[...])
        part2[chunk, :, :, FF:] = ranks.astype(BF16).reshape(SHARES, CAP, 128)

        @pl.loop(0, 4)
        def _(n):
            y = recv_g[chunk].reshape(ROWS, D_BLOCK)
            at = pl.ds(pl.multiple_of(n * 256, 256), 256)
            part2[chunk, :, :, at] = dot_nt(y, wd[at, :]).astype(BF16).reshape(SHARES, CAP, 256)

    rings = (
        (part1, ring1, rs1_send, rs1_recv, W1, CUT1),
        (part2, ring2, rs2_send, rs2_recv, W2, CUT2),
    )

    def ring_copy(stream, chunk, way, step):
        part, ring, ssem, rsem, width, cut = rings[stream]
        if step == 0:
            cols = pl.ds(0, cut) if way == 0 else pl.ds(cut, width - cut)
            src = part.at[chunk, (z + 4) % N_DP, :, cols]
            dst = ring.at[chunk, way, 0, :, cols]
        else:
            src, dst = ring.at[chunk, way, step - 1], ring.at[chunk, way, step]
        return pltpu.make_async_remote_copy(
            src, dst, ssem.at[chunk, way, step], rsem.at[chunk, way, step],
            device_id=(right if way == 0 else left, e), device_id_type=MESH,
        )

    def ring_start(stream, chunk):
        for way in range(2):
            ring_copy(stream, chunk, way, 0).start()

    def ring_step(stream, chunk, step):
        part, ring, _, _, width, cut = rings[stream]
        for way in range(2):
            ring_copy(stream, chunk, way, step - 1).wait_recv()
            target = (z + 4 - step) % N_DP if way == 0 else (z + 4 + step) % N_DP
            if step == 1:
                lo, hi = (0, cut) if way == 0 else (cut, width)
                total = ring[chunk, way, 0, :, lo:hi].astype(F32) + part[chunk, target, :, lo:hi].astype(F32)
                ring[chunk, way, 0, :, lo:hi] = total.astype(BF16)
                lo, hi = (cut, width) if way == 0 else (0, cut)
                ring[chunk, way, 0, :, lo:hi] = part[chunk, target, :, lo:hi]
            else:
                total = ring[chunk, way, step - 1].astype(F32) + part[chunk, target].astype(F32)
                ring[chunk, way, step - 1] = total.astype(BF16)
            ring_copy(stream, chunk, way, step).start()

    def ring_end(stream, chunk):
        for way in range(2):
            ring_copy(stream, chunk, way, 3).wait_recv()

    def gather_copy(chunk, way, step, arriving=False):
        hops = step + 1 if arriving else step
        owner = (z + N_DP - hops) % N_DP if way == 0 else (z + hops) % N_DP
        if step == 3:
            cols = pl.ds(0, CUTA) if way == 0 else pl.ds(CUTA, WA - CUTA)
        else:
            cols = pl.ds(0, WA)
        ref = gathered.at[chunk, owner, :, cols]
        return pltpu.make_async_remote_copy(
            ref, ref, ag_send.at[chunk, way, step], ag_recv.at[chunk, way, step],
            device_id=(right if way == 0 else left, e), device_id_type=MESH,
        )

    def gather_start(chunk):
        for way in range(2):
            gather_copy(chunk, way, 0).start()

    def gather_step(chunk, step):
        for way in range(2):
            gather_copy(chunk, way, step - 1, True).wait_recv()
            gather_copy(chunk, way, step).start()

    def gather_end(chunk):
        for way in range(2):
            gather_copy(chunk, way, 3, True).wait_recv()

    def hidden_chunk(chunk):
        at = pl.ds(FF, 128)
        ranks = (
            part2[chunk, z, :, at].astype(F32)
            + ring2[chunk, 0, 3, :, at].astype(F32)
            + ring2[chunk, 1, 3, :, at].astype(F32)
        )
        scaled = ranks * scale_row[0:1, :]
        high = scaled.astype(BF16)
        low = (scaled - high.astype(F32)).astype(BF16)
        both = jnp.concatenate([high, low], axis=0)

        def tile(n, back):
            at = pl.ds(pl.multiple_of(n * 256, 256), 256)
            at_up = pl.ds(pl.multiple_of(n * 256 + FF, 256), 256)
            at_down = pl.ds(pl.multiple_of(n * 256 + 2 * FF, 256), 256)

            def low_rank(cols):
                extra = dot_nn(both, q_all[:, cols])
                return extra[:CAP] + extra[CAP:]

            def summed(part, ring, cols):
                return (
                    part[chunk, z, :, cols].astype(F32)
                    + ring[chunk, 0, 3, :, cols].astype(F32)
                    + ring[chunk, 1, 3, :, cols].astype(F32)
                )

            gate_pre = summed(part1, ring1, at) + low_rank(at)
            up_pre = summed(part1, ring1, at_up) + low_rank(at_up)
            hidden_grad = summed(part2, ring2, at) + low_rank(at_down)
            sigmoid = 1.0 / (1.0 + jnp.exp(-gate_pre))
            activated = gate_pre * sigmoid
            slope = sigmoid * (1.0 + gate_pre * (1.0 - sigmoid))
            hidden = (activated * up_pre).astype(BF16)
            gate_grad = (hidden_grad * up_pre * slope).astype(BF16)
            up_grad = (hidden_grad * activated).astype(BF16)
            hidden_own[:, at] = hidden
            gathered[chunk, z, :, at] = gate_grad
            gathered[chunk, z, :, at_up] = up_grad
            back = back + dot_nt(gate_grad, q_all[:, at])
            back = back + dot_nt(up_grad, q_all[:, at_up])
            return back + dot_nt(hidden, q_all[:, at_down])

        back = lax.fori_loop(0, 4, tile, jnp.zeros((CAP, 128), F32))
        lane = lax.broadcasted_iota(jnp.int32, (CAP, 128), 1)
        side = jnp.where(lane < 64, back * scale_row[0:1, :], scaled).astype(BF16)
        gathered[chunk, z, :, pl.ds(2 * FF, 128)] = side
        gather_start(chunk)
        acc_lam[...] += jnp.sum(ranks * back, axis=0, keepdims=True)
        acc_pd[...] += dot_tn(side, hidden_own[...])[96:112]

    def back_chunk(chunk):
        side = gathered[chunk, :, :, pl.ds(2 * FF, 128)].reshape(ROWS, 128)
        gate_grad = gathered[chunk, :, :, pl.ds(0, FF)].reshape(ROWS, FF)
        up_grad = gathered[chunk, :, :, pl.ds(FF, FF)].reshape(ROWS, FF)
        total = dot_nt(gate_grad, wg[...]) + dot_nt(up_grad, wu[...]) + dot_nn(side[:, :64], p_tok[:64])
        route_out[chunk] = total.astype(BF16).reshape(SHARES, CAP, D_BLOCK)
        send_all(chunk, r_copy, route_out, returned, r_recv)

    def small_chunk(chunk):
        side = gathered[chunk, :, :, pl.ds(2 * FF, 128)].reshape(ROWS, 128)
        grad_p = dot_tn(side, recv_t[chunk].reshape(ROWS, D_BLOCK))
        gp_ref[0, 0] += grad_p[0:16]
        gp_ref[0, 1] += grad_p[16:32]
        gqd_ref[0] += dot_tn(side, recv_g[chunk].reshape(ROWS, D_BLOCK))[32:48]
        mine = pl.multiple_of(z * 128, 128)
        gate_mine = gathered[chunk, :, :, pl.ds(mine, 128)].reshape(ROWS, 128)
        up_mine = gathered[chunk, :, :, pl.ds(mine + FF, 128)].reshape(ROWS, 128)
        gq_ref[0, 0] += dot_tn(side, gate_mine)[64:80]
        gq_ref[0, 1] += dot_tn(side, up_mine)[80:96]

    def combine_chunk(chunk):
        wait_chunk(returned, r_recv, chunk)
        acc_in[...] += dot_tn(hot[chunk], returned[chunk].reshape(ROWS, D_BLOCK))

    p_tok[...] = jnp.zeros_like(p_tok)
    p_grad[...] = jnp.zeros_like(p_grad)
    for base in (0, 64):
        p_tok[base:base + 16, :] = p_in_ref[0, 0]
        p_tok[base + 16:base + 32, :] = p_in_ref[0, 1]
        p_grad[base + 32:base + 48, :] = q_down_ref[0]

    loads[0].wait()
    loads[1].wait()
    pl.semaphore_wait(barrier, N_EXPERT - 1 + N_DP - 1)

    @pl.loop(0, CHUNKS)
    def _(chunk):
        route_chunk(chunk)

    q_all[...] = jnp.zeros_like(q_all)
    q_all[0:16, 0:FF] = q_in_ref[0, 0]
    q_all[16:32, FF:2 * FF] = q_in_ref[0, 1]
    q_all[32:48, 2 * FF:] = p_down_ref[0]
    spread = (
        lax.broadcasted_iota(jnp.int32, (RANK, 128), 0) == lax.broadcasted_iota(jnp.int32, (RANK, 128), 1) % 16
    ).astype(F32)
    scale = lam_ref[0] * mask_ref[0].astype(F32)
    lanes = lax.broadcasted_iota(jnp.int32, (3, 128), 1)
    rows3 = lax.broadcasted_iota(jnp.int32, (3, 128), 0)
    wide = jnp.where((lanes % 64) // 16 == rows3, dot_nn(scale, spread, HIGH), 0.0)
    scale_row[0:1, :] = jnp.sum(wide, axis=0, keepdims=True)
    acc_in[...] = jnp.zeros_like(acc_in)
    acc_pd[...] = jnp.zeros_like(acc_pd)
    acc_lam[...] = jnp.zeros_like(acc_lam)
    gq_ref[...] = jnp.zeros_like(gq_ref)
    gp_ref[...] = jnp.zeros_like(gp_ref)
    gqd_ref[...] = jnp.zeros_like(gqd_ref)
    loads[2].wait()
    loads[3].wait()
    loads[4].wait()

    forward1(0)
    ring_start(0, 0)
    forward2(0)
    ring_start(1, 0)

    @pl.loop(0, CHUNKS + 1)
    def _(i):
        ringing = i < CHUNKS
        gathering = i > 0
        more = i < CHUNKS - 1
        for step in range(1, 4):
            @pl.when(ringing)
            def _():
                ring_step(0, i, step)

            @pl.when(gathering)
            def _():
                gather_step(i - 1, step)

            @pl.when(ringing)
            def _():
                ring_step(1, i, step)

            if step == 1:
                @pl.when(more)
                def _():
                    forward1(i + 1)
            if step == 2:
                @pl.when(more)
                def _():
                    forward2(i + 1)

                @pl.when(i > 1)
                def _():
                    small_chunk(i - 2)
            if step == 3:
                @pl.when(more)
                def _():
                    ring_start(0, i + 1)
                    ring_start(1, i + 1)

                @pl.when(i > 1)
                def _():
                    combine_chunk(i - 2)

        @pl.when(ringing)
        def _():
            ring_end(0, i)
            ring_end(1, i)
            hidden_chunk(i)

        @pl.when(gathering)
        def _():
            gather_end(i - 1)
            back_chunk(i - 1)

    def fin_copy(k):
        peer = (z + k) % N_DP
        return pltpu.make_async_remote_copy(
            fin_send.at[peer], fin_recv.at[k], fin_ssem.at[k], fin_rsem.at[k],
            device_id=(peer, e), device_id_type=MESH,
        )

    for k in range(N_DP):
        fin_send[k, 0:16, :] = acc_pd[:, k * 128:(k + 1) * 128]
        fin_send[k, 16:24, :] = jnp.broadcast_to(acc_lam[...], (8, 128))
    for k in range(1, N_DP):
        fin_copy(k).start()
    small_chunk(CHUNKS - 1)
    for k in range(1, N_DP):
        fin_copy(k).wait_recv()
    fin_recv[0] = fin_send[z]
    total = fin_recv[z]
    for k in range(1, N_DP):
        total = total + fin_recv[(z + N_DP - k) % N_DP]
    gpd_ref[0] = total[0:16]
    lam_total = jnp.where(lanes // 16 == rows3, jnp.broadcast_to(total[16:17], (3, 128)), 0.0)
    gl_ref[0] = dot_nt(lam_total, spread, HIGH) * mask_ref[0].astype(F32)
    combine_chunk(CHUNKS - 1)
    in_grad_ref[...] = acc_in[...].astype(BF16)

    for k in range(1, N_DP):
        fin_copy(k).wait_send()

    @pl.loop(0, CHUNKS)
    def _(chunk):
        for ref, sem in ((send_t, t_send), (send_g, g_send), (route_out, r_send)):
            @pl.when(chunk > 0)
            def _():
                pltpu.make_async_copy(ref.at[chunk], ref.at[chunk], sem.at[chunk]).wait()

            @pl.when(chunk == 0)
            def _():
                sent = ref.at[chunk, pl.ds(1, SHARES - 1)]
                pltpu.make_async_copy(sent, sent, sem.at[chunk]).wait()
        for step in range(4):
            for way in range(2):
                ring_copy(0, chunk, way, step).wait_send()
                ring_copy(1, chunk, way, step).wait_send()
                gather_copy(chunk, way, step).wait_send()


def body(
    tokens, out_grad, routes, route_weights, w_gate, w_up, w_down, p_in, q_in, p_down, q_down, lam, rank_mask
):
    vmem = pl.BlockSpec(memory_space=pltpu.VMEM)
    hbm = pl.BlockSpec(memory_space=pl.ANY)
    dma = pltpu.SemaphoreType.DMA
    grid_rows = (CHUNKS, SHARES, CAP)
    scratch = [
        pltpu.VMEM((TOK, D_BLOCK), BF16),
        pltpu.VMEM((TOK, D_BLOCK), BF16),
        pltpu.VMEM((D_BLOCK, FF), BF16),
        pltpu.VMEM((D_BLOCK, FF), BF16),
        pltpu.VMEM((FF, D_BLOCK), BF16),
        pltpu.VMEM((128, D_BLOCK), BF16),
        pltpu.VMEM((128, D_BLOCK), BF16),
        pltpu.VMEM((128, 3 * FF), BF16),
        pltpu.VMEM((CHUNKS, ROWS, TOK), BF16),
        pltpu.VMEM(grid_rows + (D_BLOCK,), BF16),
        pltpu.VMEM(grid_rows + (D_BLOCK,), BF16),
        pltpu.VMEM(grid_rows + (D_BLOCK,), BF16),
        pltpu.VMEM(grid_rows + (D_BLOCK,), BF16),
        pltpu.VMEM(grid_rows + (W1,), BF16),
        pltpu.VMEM(grid_rows + (W2,), BF16),
        pltpu.VMEM((CHUNKS, 2, 4, CAP, W1), BF16),
        pltpu.VMEM((CHUNKS, 2, 4, CAP, W2), BF16),
        pltpu.VMEM(grid_rows + (WA,), BF16),
        pltpu.VMEM(grid_rows + (D_BLOCK,), BF16),
        pltpu.VMEM(grid_rows + (D_BLOCK,), BF16),
        pltpu.VMEM((ROWS, 128), F32),
        pltpu.VMEM((CAP, FF), BF16),
        pltpu.VMEM((TOK, D_BLOCK), F32),
        pltpu.VMEM((RANK, FF), F32),
        pltpu.VMEM((1, 128), F32),
        pltpu.VMEM((1, 128), F32),
        pltpu.VMEM((2, TOK), F32),
        pltpu.VMEM((N_DP, 24, 128), F32),
        pltpu.VMEM((N_DP, 24, 128), F32),
        dma((5,)),
        dma((CHUNKS,)),
        dma((CHUNKS,)),
        dma((CHUNKS,)),
        dma((CHUNKS,)),
        dma((CHUNKS,)),
        dma((CHUNKS,)),
        dma((CHUNKS, 2, 4)),
        dma((CHUNKS, 2, 4)),
        dma((CHUNKS, 2, 4)),
        dma((CHUNKS, 2, 4)),
        dma((CHUNKS, 2, 4)),
        dma((CHUNKS, 2, 4)),
        dma((N_DP,)),
        dma((N_DP,)),
    ]
    return pl.pallas_call(
        kernel,
        out_shape=(
            jax.ShapeDtypeStruct((TOK, D_BLOCK), BF16),
            jax.ShapeDtypeStruct((1, 2, RANK, FF // N_DP), F32),
            jax.ShapeDtypeStruct((1, 2, RANK, D_BLOCK), F32),
            jax.ShapeDtypeStruct((1, RANK, FF // N_DP), F32),
            jax.ShapeDtypeStruct((1, RANK, D_BLOCK), F32),
            jax.ShapeDtypeStruct((1, 3, RANK), F32),
        ),
        in_specs=[vmem, vmem, hbm, hbm, hbm, hbm, hbm, vmem, vmem, vmem, vmem, vmem, vmem],
        out_specs=(vmem,) * 6,
        scratch_shapes=scratch,
        compiler_params=pltpu.CompilerParams(
            collective_id=0, has_side_effects=True, vmem_limit_bytes=58 * 1024 * 1024
        ),
        name="adapter_backward",
    )(
        routes.T, route_weights.T, tokens, out_grad, w_gate, w_up, w_down, p_in, q_in, p_down, q_down, lam, rank_mask
    )


def solution(mesh):
    in_specs = (
        P("expert", "dp"),
        P("expert", "dp"),
        P("expert", None),
        P("expert", None),
        P("expert", "dp", None),
        P("expert", "dp", None),
        P("expert", None, "dp"),
        P("expert", None, None, "dp"),
        P("expert", None, None, None),
        P("expert", None, None),
        P("expert", None, "dp"),
        P("expert", None, None),
        P("expert", None, None),
    )
    out_specs = (
        P("expert", "dp"),
        P("expert", None, None, "dp"),
        P("expert", None, None, "dp"),
        P("expert", None, "dp"),
        P("expert", None, "dp"),
        P("expert", None, None),
    )
    return jax.shard_map(body, mesh=mesh, in_specs=in_specs, out_specs=out_specs, check_vma=False)
```

```python
import functools

import jax
import jax.numpy as jnp
from jax import lax
from jax.experimental import pallas as pl
from jax.experimental.pallas import tpu as pltpu
from jax.sharding import PartitionSpec as P

MESH = pl.DeviceIdType.MESH
F32 = jnp.float32
BF16 = jnp.bfloat16
HIGH = lax.Precision.HIGHEST

D_BLOCK = 896
FF = 1024
RANK = 16
TOK = 256
CAP = 32
N_DP = 8
N_EXPERT = 32
CHUNKS = 4
SHARES = 8
ROWS = SHARES * CAP
WIDTHS = (FF, FF, FF + 128)
CUTS = (512, 512, 640)
HALVES = (FF, FF + 128)
WA = 2 * FF + 128
OFFSETS = (
    ((0, 0), (1, 0), (3, 0), (0, 1)),
    ((1, 1), (3, 3), (3, 1), (1, 3)),
    ((2, 1), (2, 3), (0, 2), (2, 2)),
    ((1, 2), (3, 2), (0, 3), (2, 0)),
)


def dot_nn(a, b, precision=None):
    return lax.dot_general(a, b, (((1,), (0,)), ((), ())), precision=precision, preferred_element_type=F32)


def dot_nt(a, b, precision=None):
    return lax.dot_general(a, b, (((1,), (1,)), ((), ())), precision=precision, preferred_element_type=F32)


def dot_tn(a, b):
    return lax.dot_general(a, b, (((0,), (0,)), ((), ())), preferred_element_type=F32)


def pick(values, chunk):
    if isinstance(chunk, int):
        return values[chunk]
    out = values[0]
    for k in range(1, len(values)):
        out = jnp.where(chunk == k, values[k], out)
    return out


def kernel(
    routes_ref,
    weights_ref,
    tokens_hbm,
    grads_hbm,
    wg_hbm,
    wu_hbm,
    wd_hbm,
    p_in_ref,
    q_in_ref,
    p_down_ref,
    q_down_ref,
    lam_ref,
    mask_ref,
    in_grad_ref,
    gq_ref,
    gp_ref,
    gpd_ref,
    gqd_ref,
    gl_ref,
    tok,
    out_grad,
    wg,
    wu,
    wd,
    p_tok,
    p_grad,
    q_all,
    hot,
    send_t,
    send_g,
    recv_t,
    recv_g,
    part_gate,
    part_up,
    part_down,
    ring_gate,
    ring_up,
    ring_down,
    gathered,
    route_out,
    returned,
    hidden_own,
    acc_in,
    acc_pd,
    acc_lam,
    scale_row,
    pos,
    fin_send,
    fin_recv,
    load_sem,
    t_send,
    t_recv,
    g_send,
    g_recv,
    r_send,
    r_recv,
    rs_send,
    rs_recv,
    ag_send,
    ag_recv,
    fin_ssem,
    fin_rsem,
):
    z = lax.axis_index("dp")
    e = lax.axis_index("expert")
    ex = e // 8
    ey = (e // 2) % 4
    ec = e % 2
    right = (z + 1) % N_DP
    left = (z + N_DP - 1) % N_DP

    def expert_at(chunk, j, sign):
        dx = pick([o[j // 2][0] for o in OFFSETS], chunk)
        dy = pick([o[j // 2][1] for o in OFFSETS], chunk)
        x = (ex + 4 + sign * dx) % 4
        y = (ey + 4 + sign * dy) % 4
        return (x * 4 + y) * 2 + (ec + j) % 2

    loads = []
    for k, (src, dst) in enumerate(
        (
            (tokens_hbm, tok),
            (grads_hbm, out_grad),
            (wg_hbm.at[0], wg),
            (wu_hbm.at[0], wu),
            (wd_hbm.at[0], wd),
        )
    ):
        copy = pltpu.make_async_copy(src, dst, load_sem.at[k])
        copy.start()
        loads.append(copy)

    barrier = pltpu.get_barrier_semaphore()
    for k in range(1, N_EXPERT):
        pl.semaphore_signal(barrier, inc=1, device_id=(z, (e + k) % N_EXPERT), device_id_type=MESH)
    for k in range(1, N_DP):
        pl.semaphore_signal(barrier, inc=1, device_id=((z + k) % N_DP, e), device_id_type=MESH)

    expert_iota = lax.broadcasted_iota(jnp.int32, (N_EXPERT, TOK), 0)
    named0 = (expert_iota == routes_ref[0:1, :]).astype(F32)
    named1 = (expert_iota == routes_ref[1:2, :]).astype(F32)
    earlier = (
        lax.broadcasted_iota(jnp.int32, (TOK, TOK), 0) < lax.broadcasted_iota(jnp.int32, (TOK, TOK), 1)
    ).astype(BF16)
    before = dot_nn((named0 + named1).astype(BF16), earlier)
    pos[0:1, :] = jnp.sum(named0 * before, axis=0, keepdims=True) + CAP * routes_ref[0:1, :].astype(F32)
    pos[1:2, :] = jnp.sum(named1 * before, axis=0, keepdims=True) + CAP * routes_ref[1:2, :].astype(F32)

    def t_copy(chunk, j):
        return pltpu.make_async_remote_copy(
            send_t.at[chunk, j], recv_t.at[chunk, j], t_send.at[chunk], t_recv.at[chunk],
            device_id=(z, expert_at(chunk, j, -1)), device_id_type=MESH,
        )

    def g_copy(chunk, j):
        return pltpu.make_async_remote_copy(
            send_g.at[chunk, j], recv_g.at[chunk, j], g_send.at[chunk], g_recv.at[chunk],
            device_id=(z, expert_at(chunk, j, -1)), device_id_type=MESH,
        )

    def r_copy(chunk, j):
        return pltpu.make_async_remote_copy(
            route_out.at[chunk, j], returned.at[chunk, j], r_send.at[chunk], r_recv.at[chunk],
            device_id=(z, expert_at(chunk, j, 1)), device_id_type=MESH,
        )

    def send_all(chunk, copy_of, src, dst, sem):
        for j in range(SHARES):
            if j == 0:
                @pl.when(chunk > 0)
                def _():
                    copy_of(chunk, 0).start()

                @pl.when(chunk == 0)
                def _():
                    pltpu.make_async_copy(src.at[chunk, 0], dst.at[chunk, 0], sem.at[chunk]).start()
            else:
                copy_of(chunk, j).start()

    def wait_chunk(ref, sem, chunk):
        pltpu.make_async_copy(ref.at[chunk], ref.at[chunk], sem.at[chunk]).wait()

    slot_iota = lax.broadcasted_iota(jnp.int32, (CAP, TOK), 0)

    def route_chunk(chunk):
        pos0, pos1 = pos[0:1, :], pos[1:2, :]
        weight0, weight1 = weights_ref[0:1, :], weights_ref[1:2, :]
        slot_weights = []
        for j in range(SHARES):
            target = (slot_iota + CAP * expert_at(chunk, j, -1)).astype(F32)
            hit0, hit1 = target == pos0, target == pos1
            hot[chunk, j * CAP:(j + 1) * CAP, :] = jnp.where(hit0 | hit1, 1.0, 0.0).astype(BF16)
            weight = jnp.where(hit0, weight0, 0.0) + jnp.where(hit1, weight1, 0.0)
            slot_weights.append(jnp.sum(weight, axis=1, keepdims=True))
        picked = dot_nn(hot[chunk], tok[...])
        send_t[chunk] = picked.astype(BF16).reshape(SHARES, CAP, D_BLOCK)
        picked = dot_nn(hot[chunk], out_grad[...])
        for j in range(SHARES):
            send_g[chunk, j] = (slot_weights[j] * picked[j * CAP:(j + 1) * CAP, :]).astype(BF16)

    def route_send(chunk):
        send_all(chunk, t_copy, send_t, recv_t, t_recv)
        send_all(chunk, g_copy, send_g, recv_g, g_recv)

    def project(chunk, source, weights, part, transposed=False):
        @pl.loop(0, 2)
        def _(n):
            x = source[chunk].reshape(ROWS, D_BLOCK)
            at = pl.ds(pl.multiple_of(n * 512, 512), 512)
            out = dot_nt(x, weights[at, :]) if transposed else dot_nn(x, weights[:, at])
            part[chunk, :, :, at] = out.astype(BF16).reshape(SHARES, CAP, 512)

    def forward_gate(chunk):
        wait_chunk(recv_t, t_recv, chunk)
        project(chunk, recv_t, wg, part_gate)

    def forward_up(chunk):
        project(chunk, recv_t, wu, part_up)

    def forward_down(chunk):
        wait_chunk(recv_g, g_recv, chunk)
        ranks = dot_nt(recv_t[chunk].reshape(ROWS, D_BLOCK), p_tok[...])
        ranks = ranks + dot_nt(recv_g[chunk].reshape(ROWS, D_BLOCK), p_grad[...])
        part_down[chunk, :, :, pl.ds(FF, 128)] = ranks.astype(BF16).reshape(SHARES, CAP, 128)
        project(chunk, recv_g, wd, part_down, True)

    rings = ((part_gate, ring_gate), (part_up, ring_up), (part_down, ring_down))

    def ring_copy(stream, chunk, way, step):
        part, ring = rings[stream]
        width, cut = WIDTHS[stream], CUTS[stream]
        if step == 0:
            cols = pl.ds(0, cut) if way == 0 else pl.ds(cut, width - cut)
            src = part.at[chunk, (z + 4) % N_DP, :, cols]
            dst = ring.at[chunk, way, 0, :, cols]
        else:
            src, dst = ring.at[chunk, way, step - 1], ring.at[chunk, way, step]
        return pltpu.make_async_remote_copy(
            src, dst, rs_send.at[stream, way, step], rs_recv.at[stream, way, step],
            device_id=(right if way == 0 else left, e), device_id_type=MESH,
        )

    def start_next(copy, chunk):
        if not (isinstance(chunk, int) and chunk == 0):
            @pl.when(chunk > 0)
            def _():
                copy.wait_send()

        copy.start()

    def ring_start(stream, chunk):
        for way in range(2):
            start_next(ring_copy(stream, chunk, way, 0), chunk)

    def ring_step(stream, chunk, step):
        part, ring = rings[stream]
        width, cut = WIDTHS[stream], CUTS[stream]
        for way in range(2):
            ring_copy(stream, chunk, way, step - 1).wait_recv()
            target = (z + 4 - step) % N_DP if way == 0 else (z + 4 + step) % N_DP
            if step == 1:
                lo, hi = (0, cut) if way == 0 else (cut, width)
                total = ring[chunk, way, 0, :, lo:hi].astype(F32) + part[chunk, target, :, lo:hi].astype(F32)
                ring[chunk, way, 0, :, lo:hi] = total.astype(BF16)
                lo, hi = (cut, width) if way == 0 else (0, cut)
                ring[chunk, way, 0, :, lo:hi] = part[chunk, target, :, lo:hi]
            else:
                total = ring[chunk, way, step - 1].astype(F32) + part[chunk, target].astype(F32)
                ring[chunk, way, step - 1] = total.astype(BF16)
            start_next(ring_copy(stream, chunk, way, step), chunk)

    def ring_end(chunk):
        for stream in range(3):
            for way in range(2):
                ring_copy(stream, chunk, way, 3).wait_recv()

    def gather_copy(half, chunk, way, step, arriving=False):
        hops = step + 1 if arriving else step
        owner = (z + N_DP - hops) % N_DP if way == 0 else (z + hops) % N_DP
        ref = gathered.at[chunk, owner, :, pl.ds(half * FF, HALVES[half])]
        return pltpu.make_async_remote_copy(
            ref, ref, ag_send.at[half, way, step], ag_recv.at[half, way, step],
            device_id=(right if way == 0 else left, e), device_id_type=MESH,
        )

    def gather_ways(half, step):
        return (half,) if step == 3 else (0, 1)

    def gather_start(chunk):
        for half in range(2):
            for way in range(2):
                start_next(gather_copy(half, chunk, way, 0), chunk)

    def gather_step(half, chunk, step):
        for way in range(2):
            gather_copy(half, chunk, way, step - 1, True).wait_recv()
            if way in gather_ways(half, step):
                start_next(gather_copy(half, chunk, way, step), chunk)

    def gather_end(chunk):
        for half in range(2):
            gather_copy(half, chunk, half, 3, True).wait_recv()

    def hidden_chunk(chunk):
        at = pl.ds(FF, 128)
        ranks = (
            part_down[chunk, z, :, at].astype(F32)
            + ring_down[chunk, 0, 3, :, at].astype(F32)
            + ring_down[chunk, 1, 3, :, at].astype(F32)
        )
        scaled = ranks * scale_row[0:1, :]
        high = scaled.astype(BF16)
        low = (scaled - high.astype(F32)).astype(BF16)
        both = jnp.concatenate([high, low], axis=0)

        def tile(n, back):
            at = pl.ds(pl.multiple_of(n * 256, 256), 256)
            at_up = pl.ds(pl.multiple_of(n * 256 + FF, 256), 256)
            at_down = pl.ds(pl.multiple_of(n * 256 + 2 * FF, 256), 256)

            def low_rank(cols):
                extra = dot_nn(both, q_all[:, cols])
                return extra[:CAP] + extra[CAP:]

            def summed(part, ring, cols):
                return (
                    part[chunk, z, :, cols].astype(F32)
                    + ring[chunk, 0, 3, :, cols].astype(F32)
                    + ring[chunk, 1, 3, :, cols].astype(F32)
                )

            gate_pre = summed(part_gate, ring_gate, at) + low_rank(at)
            up_pre = summed(part_up, ring_up, at) + low_rank(at_up)
            hidden_grad = summed(part_down, ring_down, at) + low_rank(at_down)
            sigmoid = 1.0 / (1.0 + jnp.exp(-gate_pre))
            activated = gate_pre * sigmoid
            slope = sigmoid * (1.0 + gate_pre * (1.0 - sigmoid))
            hidden = (activated * up_pre).astype(BF16)
            gate_grad = (hidden_grad * up_pre * slope).astype(BF16)
            up_grad = (hidden_grad * activated).astype(BF16)
            hidden_own[:, at] = hidden
            gathered[chunk, z, :, at] = gate_grad
            gathered[chunk, z, :, at_up] = up_grad
            back = back + dot_nt(gate_grad, q_all[:, at])
            back = back + dot_nt(up_grad, q_all[:, at_up])
            return back + dot_nt(hidden, q_all[:, at_down])

        back = lax.fori_loop(0, 4, tile, jnp.zeros((CAP, 128), F32))
        lane = lax.broadcasted_iota(jnp.int32, (CAP, 128), 1)
        side = jnp.where(lane < 64, back * scale_row[0:1, :], scaled).astype(BF16)
        gathered[chunk, z, :, pl.ds(2 * FF, 128)] = side
        gather_start(chunk)
        acc_lam[...] += jnp.sum(ranks * back, axis=0, keepdims=True)
        acc_pd[...] += dot_tn(side, hidden_own[...])[96:112]

    def back_chunk(chunk):
        side = gathered[chunk, :, :, pl.ds(2 * FF, 128)].reshape(ROWS, 128)
        gate_grad = gathered[chunk, :, :, pl.ds(0, FF)].reshape(ROWS, FF)
        up_grad = gathered[chunk, :, :, pl.ds(FF, FF)].reshape(ROWS, FF)
        total = dot_nt(gate_grad, wg[...]) + dot_nt(up_grad, wu[...]) + dot_nn(side[:, :64], p_tok[:64])
        route_out[chunk] = total.astype(BF16).reshape(SHARES, CAP, D_BLOCK)
        send_all(chunk, r_copy, route_out, returned, r_recv)

    def small_chunk(chunk):
        side = gathered[chunk, :, :, pl.ds(2 * FF, 128)].reshape(ROWS, 128)
        grad_p = dot_tn(side, recv_t[chunk].reshape(ROWS, D_BLOCK))
        gp_ref[0, 0] += grad_p[0:16]
        gp_ref[0, 1] += grad_p[16:32]
        gqd_ref[0] += dot_tn(side, recv_g[chunk].reshape(ROWS, D_BLOCK))[32:48]
        mine = pl.multiple_of(z * 128, 128)
        gate_mine = gathered[chunk, :, :, pl.ds(mine, 128)].reshape(ROWS, 128)
        up_mine = gathered[chunk, :, :, pl.ds(mine + FF, 128)].reshape(ROWS, 128)
        gq_ref[0, 0] += dot_tn(side, gate_mine)[64:80]
        gq_ref[0, 1] += dot_tn(side, up_mine)[80:96]

    def combine_chunk(chunk):
        wait_chunk(returned, r_recv, chunk)
        acc_in[...] += dot_tn(hot[chunk], returned[chunk].reshape(ROWS, D_BLOCK))

    p_tok[...] = jnp.zeros_like(p_tok)
    p_grad[...] = jnp.zeros_like(p_grad)
    for base in (0, 64):
        p_tok[base:base + 16, :] = p_in_ref[0, 0]
        p_tok[base + 16:base + 32, :] = p_in_ref[0, 1]
        p_grad[base + 32:base + 48, :] = q_down_ref[0]

    loads[0].wait()
    loads[1].wait()

    @pl.loop(0, CHUNKS)
    def _(chunk):
        route_chunk(chunk)

    pl.semaphore_wait(barrier, N_EXPERT - 1 + N_DP - 1)

    route_send(0)

    q_all[...] = jnp.zeros_like(q_all)
    q_all[0:16, 0:FF] = q_in_ref[0, 0]
    q_all[16:32, FF:2 * FF] = q_in_ref[0, 1]
    q_all[32:48, 2 * FF:] = p_down_ref[0]
    spread = (
        lax.broadcasted_iota(jnp.int32, (RANK, 128), 0) == lax.broadcasted_iota(jnp.int32, (RANK, 128), 1) % 16
    ).astype(F32)
    lanes = lax.broadcasted_iota(jnp.int32, (1, 128), 1)
    wide = jnp.zeros((1, 128), F32)
    for k in range(3):
        scale = lam_ref[k] * mask_ref[k].astype(F32)
        wide = wide + jnp.where((lanes % 64) // 16 == k, dot_nn(scale, spread, HIGH), 0.0)
    scale_row[...] = wide
    acc_in[...] = jnp.zeros_like(acc_in)
    acc_pd[...] = jnp.zeros_like(acc_pd)
    acc_lam[...] = jnp.zeros_like(acc_lam)
    gq_ref[...] = jnp.zeros_like(gq_ref)
    gp_ref[...] = jnp.zeros_like(gp_ref)
    gqd_ref[...] = jnp.zeros_like(gqd_ref)
    loads[2].wait()
    loads[3].wait()
    loads[4].wait()

    def fin_copy(k):
        peer = (z + k) % N_DP
        return pltpu.make_async_remote_copy(
            fin_send.at[peer], fin_recv.at[k], fin_ssem.at[k], fin_rsem.at[k],
            device_id=(peer, e), device_id_type=MESH,
        )

    wait_chunk(recv_t, t_recv, 0)
    route_send(1)
    project(0, recv_t, wg, part_gate)
    ring_start(0, 0)
    route_send(2)
    forward_up(0)
    ring_start(1, 0)
    forward_down(0)
    ring_start(2, 0)

    @pl.loop(0, CHUNKS + 1)
    def _(i):
        ringing = i < CHUNKS
        gathering = i > 0
        more = i < CHUNKS - 1
        for step in range(1, 4):
            for stream in range(3):
                @pl.when(ringing)
                def _():
                    ring_step(stream, i, step)

                if stream < 2:
                    @pl.when(gathering)
                    def _():
                        gather_step(stream, i - 1, step)

            if step == 1:
                @pl.when(i == CHUNKS)
                def _():
                    for k in range(N_DP):
                        fin_send[k, 0:16, :] = acc_pd[:, k * 128:(k + 1) * 128]
                        fin_send[k, 16:24, :] = jnp.broadcast_to(acc_lam[...], (8, 128))
                    for k in range(1, N_DP):
                        fin_copy(k).start()

                @pl.when(i > 1)
                def _():
                    back_chunk(i - 2)
                    small_chunk(i - 2)

            if step == 2:
                @pl.when(i == 0)
                def _():
                    route_send(CHUNKS - 1)

                @pl.when(more)
                def _():
                    forward_gate(i + 1)
                    forward_up(i + 1)

                @pl.when(i > 2)
                def _():
                    combine_chunk(i - 3)

            if step == 3:
                @pl.when(more)
                def _():
                    ring_start(0, i + 1)
                    ring_start(1, i + 1)
                    forward_down(i + 1)
                    ring_start(2, i + 1)

        @pl.when(ringing)
        def _():
            ring_end(i)
            hidden_chunk(i)

        @pl.when(gathering)
        def _():
            gather_end(i - 1)

    back_chunk(CHUNKS - 1)
    small_chunk(CHUNKS - 1)
    combine_chunk(CHUNKS - 2)
    for k in range(1, N_DP):
        fin_copy(k).wait_recv()
    fin_recv[0] = fin_send[z]
    total = fin_recv[z]
    for k in range(1, N_DP):
        total = total + fin_recv[(z + N_DP - k) % N_DP]
    gpd_ref[0] = total[0:16]
    for k in range(3):
        lam_total = jnp.where(lanes // 16 == k, total[16:17], 0.0)
        gl_ref[k] = dot_nt(lam_total, spread, HIGH) * mask_ref[k].astype(F32)
    combine_chunk(CHUNKS - 1)
    in_grad_ref[...] = acc_in[...].astype(BF16)

    for k in range(1, N_DP):
        fin_copy(k).wait_send()

    @pl.loop(0, CHUNKS)
    def _(chunk):
        for ref, sem in ((send_t, t_send), (send_g, g_send), (route_out, r_send)):
            @pl.when(chunk > 0)
            def _():
                pltpu.make_async_copy(ref.at[chunk], ref.at[chunk], sem.at[chunk]).wait()

            @pl.when(chunk == 0)
            def _():
                sent = ref.at[chunk, pl.ds(1, SHARES - 1)]
                pltpu.make_async_copy(sent, sent, sem.at[chunk]).wait()

    for step in range(4):
        for way in range(2):
            for stream in range(3):
                ring_copy(stream, CHUNKS - 1, way, step).wait_send()
            for half in range(2):
                if way in gather_ways(half, step):
                    gather_copy(half, CHUNKS - 1, way, step).wait_send()


def deliver(*refs):
    for k in range(6):
        refs[k + 6][...] = refs[k][...]


def body(
    tokens, out_grad, routes, route_weights, w_gate, w_up, w_down, p_in, q_in, p_down, q_down, lam, rank_mask
):
    vmem = pl.BlockSpec(memory_space=pltpu.VMEM)
    hbm = pl.BlockSpec(memory_space=pl.ANY)
    dma = pltpu.SemaphoreType.DMA
    grid_rows = (CHUNKS, SHARES, CAP)
    scratch = [
        pltpu.VMEM((TOK, D_BLOCK), BF16),
        pltpu.VMEM((TOK, D_BLOCK), BF16),
        pltpu.VMEM((D_BLOCK, FF), BF16),
        pltpu.VMEM((D_BLOCK, FF), BF16),
        pltpu.VMEM((FF, D_BLOCK), BF16),
        pltpu.VMEM((128, D_BLOCK), BF16),
        pltpu.VMEM((128, D_BLOCK), BF16),
        pltpu.VMEM((128, 3 * FF), BF16),
        pltpu.VMEM((CHUNKS, ROWS, TOK), BF16),
        pltpu.VMEM(grid_rows + (D_BLOCK,), BF16),
        pltpu.VMEM(grid_rows + (D_BLOCK,), BF16),
        pltpu.VMEM(grid_rows + (D_BLOCK,), BF16),
        pltpu.VMEM(grid_rows + (D_BLOCK,), BF16),
        *[pltpu.VMEM(grid_rows + (width,), BF16) for width in WIDTHS],
        *[pltpu.VMEM((CHUNKS, 2, 4, CAP, width), BF16) for width in WIDTHS],
        pltpu.VMEM(grid_rows + (WA,), BF16),
        pltpu.VMEM(grid_rows + (D_BLOCK,), BF16),
        pltpu.VMEM(grid_rows + (D_BLOCK,), BF16),
        pltpu.VMEM((CAP, FF), BF16),
        pltpu.VMEM((TOK, D_BLOCK), F32),
        pltpu.VMEM((RANK, FF), F32),
        pltpu.VMEM((1, 128), F32),
        pltpu.VMEM((1, 128), F32),
        pltpu.VMEM((2, TOK), F32),
        pltpu.VMEM((N_DP, 24, 128), F32),
        pltpu.VMEM((N_DP, 24, 128), F32),
        dma((5,)),
        dma((CHUNKS,)),
        dma((CHUNKS,)),
        dma((CHUNKS,)),
        dma((CHUNKS,)),
        dma((CHUNKS,)),
        dma((CHUNKS,)),
        dma((3, 2, 4)),
        dma((3, 2, 4)),
        dma((2, 2, 4)),
        dma((2, 2, 4)),
        dma((N_DP,)),
        dma((N_DP,)),
    ]
    results = pl.pallas_call(
        kernel,
        out_shape=(
            jax.ShapeDtypeStruct((TOK, D_BLOCK), BF16),
            jax.ShapeDtypeStruct((1, 2, RANK, FF // N_DP), F32),
            jax.ShapeDtypeStruct((1, 2, RANK, D_BLOCK), F32),
            jax.ShapeDtypeStruct((1, RANK, FF // N_DP), F32),
            jax.ShapeDtypeStruct((1, RANK, D_BLOCK), F32),
            jax.ShapeDtypeStruct((3, 1, RANK), F32),
        ),
        in_specs=[vmem, vmem, hbm, hbm, hbm, hbm, hbm, vmem, vmem, vmem, vmem, vmem, vmem],
        out_specs=(vmem,) * 6,
        scratch_shapes=scratch,
        compiler_params=pltpu.CompilerParams(
            collective_id=0, has_side_effects=True, vmem_limit_bytes=58 * 1024 * 1024
        ),
        name="adapter_backward",
    )(
        routes.T, route_weights.T, tokens, out_grad, w_gate, w_up, w_down, p_in, q_in, p_down, q_down,
        lam.transpose(1, 0, 2), rank_mask.transpose(1, 0, 2),
    )
    results = pl.pallas_call(
        deliver,
        out_shape=tuple(jax.ShapeDtypeStruct(r.shape, r.dtype) for r in results),
        in_specs=[vmem] * 6,
        out_specs=(vmem,) * 6,
        name="deliver",
    )(*results)
    return (*results[:5], results[5].transpose(1, 0, 2))


def solution(mesh):
    in_specs = (
        P("expert", "dp"),
        P("expert", "dp"),
        P("expert", None),
        P("expert", None),
        P("expert", "dp", None),
        P("expert", "dp", None),
        P("expert", None, "dp"),
        P("expert", None, None, "dp"),
        P("expert", None, None, None),
        P("expert", None, None),
        P("expert", None, "dp"),
        P("expert", None, None),
        P("expert", None, None),
    )
    out_specs = (
        P("expert", "dp"),
        P("expert", None, None, "dp"),
        P("expert", None, None, "dp"),
        P("expert", None, "dp"),
        P("expert", None, "dp"),
        P("expert", None, None),
    )
    return jax.shard_map(body, mesh=mesh, in_specs=in_specs, out_specs=out_specs, check_vma=False)
```

```python
import functools

import jax
import jax.numpy as jnp
from jax import lax
from jax.experimental import pallas as pl
from jax.experimental.pallas import tpu as pltpu
from jax.sharding import PartitionSpec as P

MESH = pl.DeviceIdType.MESH
F32 = jnp.float32
BF16 = jnp.bfloat16
HIGH = lax.Precision.HIGHEST

D_BLOCK = 896
FF = 1024
RANK = 16
TOK = 256
CAP = 32
N_DP = 8
N_EXPERT = 32
CHUNKS = 4
SHARES = 8
ROWS = SHARES * CAP
WIDTHS = (FF, FF, FF + 128)
CUTS = (512, 512, 640)
PIECES = (512, 512, 512, 640)
WA = 2 * FF + 128
OFFSETS = (
    ((0, 0), (1, 0), (3, 0), (0, 1)),
    ((1, 1), (3, 3), (3, 1), (1, 3)),
    ((2, 1), (2, 3), (0, 2), (2, 2)),
    ((1, 2), (3, 2), (0, 3), (2, 0)),
)


def dot_nn(a, b, precision=None):
    return lax.dot_general(a, b, (((1,), (0,)), ((), ())), precision=precision, preferred_element_type=F32)


def dot_nt(a, b, precision=None):
    return lax.dot_general(a, b, (((1,), (1,)), ((), ())), precision=precision, preferred_element_type=F32)


def dot_tn(a, b):
    return lax.dot_general(a, b, (((0,), (0,)), ((), ())), preferred_element_type=F32)


def pick(values, chunk):
    if isinstance(chunk, int):
        return values[chunk]
    out = values[0]
    for k in range(1, len(values)):
        out = jnp.where(chunk == k, values[k], out)
    return out


def kernel(
    routes_ref,
    weights_ref,
    tokens_hbm,
    grads_hbm,
    wg_hbm,
    wu_hbm,
    wd_hbm,
    p_in_ref,
    q_in_ref,
    p_down_ref,
    q_down_ref,
    lam_ref,
    mask_ref,
    in_grad_ref,
    gq_ref,
    gp_ref,
    gpd_ref,
    gqd_ref,
    gl_ref,
    tok,
    out_grad,
    wg,
    wu,
    wd,
    p_tok,
    p_grad,
    q_all,
    hot,
    send_t,
    send_g,
    recv_t,
    recv_g,
    part_gate,
    part_up,
    part_down,
    ring_gate,
    ring_up,
    ring_down,
    gathered,
    near,
    route_out,
    returned,
    hidden_own,
    acc_in,
    acc_pd,
    acc_lam,
    scale_row,
    pos,
    fin_send,
    fin_recv,
    load_sem,
    t_send,
    t_recv,
    g_send,
    g_recv,
    r_send,
    r_recv,
    rs_send,
    rs_recv,
    ag_send,
    ag_recv,
    fin_ssem,
    fin_rsem,
):
    z = lax.axis_index("dp")
    e = lax.axis_index("expert")
    ex = e // 8
    ey = (e // 2) % 4
    ec = e % 2
    right = (z + 1) % N_DP
    left = (z + N_DP - 1) % N_DP

    def expert_at(chunk, j, sign):
        dx = pick([o[j // 2][0] for o in OFFSETS], chunk)
        dy = pick([o[j // 2][1] for o in OFFSETS], chunk)
        x = (ex + 4 + sign * dx) % 4
        y = (ey + 4 + sign * dy) % 4
        return (x * 4 + y) * 2 + (ec + j) % 2

    loads = []
    for k, (src, dst) in enumerate(
        (
            (tokens_hbm, tok),
            (grads_hbm, out_grad),
            (wg_hbm.at[0], wg),
            (wu_hbm.at[0], wu),
            (wd_hbm.at[0], wd),
        )
    ):
        copy = pltpu.make_async_copy(src, dst, load_sem.at[k])
        copy.start()
        loads.append(copy)

    barrier = pltpu.get_barrier_semaphore()
    for k in range(1, N_EXPERT):
        pl.semaphore_signal(barrier, inc=1, device_id=(z, (e + k) % N_EXPERT), device_id_type=MESH)
    for k in range(1, N_DP):
        pl.semaphore_signal(barrier, inc=1, device_id=((z + k) % N_DP, e), device_id_type=MESH)

    expert_iota = lax.broadcasted_iota(jnp.int32, (N_EXPERT, TOK), 0)
    named0 = (expert_iota == routes_ref[0:1, :]).astype(F32)
    named1 = (expert_iota == routes_ref[1:2, :]).astype(F32)
    earlier = (
        lax.broadcasted_iota(jnp.int32, (TOK, TOK), 0) < lax.broadcasted_iota(jnp.int32, (TOK, TOK), 1)
    ).astype(BF16)
    before = dot_nn((named0 + named1).astype(BF16), earlier)
    pos[0:1, :] = jnp.sum(named0 * before, axis=0, keepdims=True) + CAP * routes_ref[0:1, :].astype(F32)
    pos[1:2, :] = jnp.sum(named1 * before, axis=0, keepdims=True) + CAP * routes_ref[1:2, :].astype(F32)

    def t_copy(chunk, j):
        return pltpu.make_async_remote_copy(
            send_t.at[chunk, j], recv_t.at[chunk, j], t_send.at[chunk], t_recv.at[chunk],
            device_id=(z, expert_at(chunk, j, -1)), device_id_type=MESH,
        )

    def g_copy(chunk, j):
        return pltpu.make_async_remote_copy(
            send_g.at[chunk, j], recv_g.at[chunk, j], g_send.at[chunk], g_recv.at[chunk],
            device_id=(z, expert_at(chunk, j, -1)), device_id_type=MESH,
        )

    def r_copy(chunk, j):
        return pltpu.make_async_remote_copy(
            route_out.at[chunk, j], returned.at[chunk, j], r_send.at[chunk], r_recv.at[chunk],
            device_id=(z, expert_at(chunk, j, 1)), device_id_type=MESH,
        )

    def send_all(chunk, copy_of, src, dst, sem):
        for j in range(SHARES):
            if j == 0:
                @pl.when(chunk > 0)
                def _():
                    copy_of(chunk, 0).start()

                @pl.when(chunk == 0)
                def _():
                    pltpu.make_async_copy(src.at[chunk, 0], dst.at[chunk, 0], sem.at[chunk]).start()
            else:
                copy_of(chunk, j).start()

    def wait_chunk(ref, sem, chunk):
        pltpu.make_async_copy(ref.at[chunk], ref.at[chunk], sem.at[chunk]).wait()

    slot_iota = lax.broadcasted_iota(jnp.int32, (CAP, TOK), 0)

    def route_chunk(chunk):
        pos0, pos1 = pos[0:1, :], pos[1:2, :]
        weight0, weight1 = weights_ref[0:1, :], weights_ref[1:2, :]
        slot_weights = []
        for j in range(SHARES):
            target = (slot_iota + CAP * expert_at(chunk, j, -1)).astype(F32)
            hit0, hit1 = target == pos0, target == pos1
            hot[chunk, j * CAP:(j + 1) * CAP, :] = jnp.where(hit0 | hit1, 1.0, 0.0).astype(BF16)
            weight = jnp.where(hit0, weight0, 0.0) + jnp.where(hit1, weight1, 0.0)
            slot_weights.append(jnp.sum(weight, axis=1, keepdims=True))
        picked = dot_nn(hot[chunk], tok[...])
        send_t[chunk] = picked.astype(BF16).reshape(SHARES, CAP, D_BLOCK)
        picked = dot_nn(hot[chunk], out_grad[...])
        for j in range(SHARES):
            send_g[chunk, j] = (slot_weights[j] * picked[j * CAP:(j + 1) * CAP, :]).astype(BF16)

    def route_send(chunk):
        send_all(chunk, t_copy, send_t, recv_t, t_recv)
        send_all(chunk, g_copy, send_g, recv_g, g_recv)

    def project(chunk, source, weights, part, transposed=False):
        @pl.loop(0, 2)
        def _(n):
            x = source[chunk].reshape(ROWS, D_BLOCK)
            at = pl.ds(pl.multiple_of(n * 512, 512), 512)
            out = dot_nt(x, weights[at, :]) if transposed else dot_nn(x, weights[:, at])
            part[chunk, :, :, at] = out.astype(BF16).reshape(SHARES, CAP, 512)

    def forward_gate(chunk):
        wait_chunk(recv_t, t_recv, chunk)
        project(chunk, recv_t, wg, part_gate)

    def forward_up(chunk):
        project(chunk, recv_t, wu, part_up)

    def forward_down(chunk):
        wait_chunk(recv_g, g_recv, chunk)
        ranks = dot_nt(recv_t[chunk].reshape(ROWS, D_BLOCK), p_tok[...])
        ranks = ranks + dot_nt(recv_g[chunk].reshape(ROWS, D_BLOCK), p_grad[...])
        part_down[chunk, :, :, pl.ds(FF, 128)] = ranks.astype(BF16).reshape(SHARES, CAP, 128)
        project(chunk, recv_g, wd, part_down, True)

    rings = ((part_gate, ring_gate), (part_up, ring_up), (part_down, ring_down))

    def ring_copy(stream, chunk, way, step):
        part, ring = rings[stream]
        width, cut = WIDTHS[stream], CUTS[stream]
        if step == 0:
            cols = pl.ds(0, cut) if way == 0 else pl.ds(cut, width - cut)
            src = part.at[chunk, (z + 4) % N_DP, :, cols]
            dst = ring.at[chunk, way, 0, :, cols]
        else:
            src, dst = ring.at[chunk, way, step - 1], ring.at[chunk, way, step]
        return pltpu.make_async_remote_copy(
            src, dst, rs_send.at[stream, way, step], rs_recv.at[stream, way, step],
            device_id=(right if way == 0 else left, e), device_id_type=MESH,
        )

    def start_next(copy, chunk):
        if not (isinstance(chunk, int) and chunk == 0):
            @pl.when(chunk > 0)
            def _():
                copy.wait_send()

        copy.start()

    def ring_start(stream, chunk):
        for way in range(2):
            start_next(ring_copy(stream, chunk, way, 0), chunk)

    def ring_step(stream, chunk, step):
        part, ring = rings[stream]
        width, cut = WIDTHS[stream], CUTS[stream]
        for way in range(2):
            ring_copy(stream, chunk, way, step - 1).wait_recv()
            target = (z + 4 - step) % N_DP if way == 0 else (z + 4 + step) % N_DP
            if step == 1:
                lo, hi = (0, cut) if way == 0 else (cut, width)
                total = ring[chunk, way, 0, :, lo:hi].astype(F32) + part[chunk, target, :, lo:hi].astype(F32)
                ring[chunk, way, 0, :, lo:hi] = total.astype(BF16)
                lo, hi = (cut, width) if way == 0 else (0, cut)
                ring[chunk, way, 0, :, lo:hi] = part[chunk, target, :, lo:hi]
            else:
                total = ring[chunk, way, step - 1].astype(F32) + part[chunk, target].astype(F32)
                ring[chunk, way, step - 1] = total.astype(BF16)
            start_next(ring_copy(stream, chunk, way, step), chunk)

    def ring_end(chunk):
        for stream in range(3):
            for way in range(2):
                ring_copy(stream, chunk, way, 3).wait_recv()

    def gather_copy(half, chunk, way, step, arriving=False):
        hops = step + 1 if arriving else step
        owner = (z + N_DP - hops) % N_DP if way == 0 else (z + hops) % N_DP
        ref = gathered.at[chunk, owner, :, pl.ds(half * 512, PIECES[half])]
        return pltpu.make_async_remote_copy(
            ref, ref, ag_send.at[half, way, step], ag_recv.at[half, way, step],
            device_id=(right if way == 0 else left, e), device_id_type=MESH,
        )

    def gather_ways(half, step):
        return (half // 2,) if step == 3 else (0, 1)

    def gather_start(chunk, pieces):
        for half in pieces:
            for way in range(2):
                start_next(gather_copy(half, chunk, way, 0), chunk)

    def gather_step(half, chunk, step):
        for way in range(2):
            gather_copy(half, chunk, way, step - 1, True).wait_recv()
            if way in gather_ways(half, step):
                start_next(gather_copy(half, chunk, way, step), chunk)

    def gather_end(chunk):
        for half in range(4):
            gather_copy(half, chunk, half // 2, 3, True).wait_recv()

    def hidden_chunk(chunk):
        at = pl.ds(FF, 128)
        ranks = (
            part_down[chunk, z, :, at].astype(F32)
            + ring_down[chunk, 0, 3, :, at].astype(F32)
            + ring_down[chunk, 1, 3, :, at].astype(F32)
        )
        scaled = ranks * scale_row[0:1, :]
        high = scaled.astype(BF16)
        low = (scaled - high.astype(F32)).astype(BF16)
        both = jnp.concatenate([high, low], axis=0)

        def tile(n, back):
            at = pl.ds(pl.multiple_of(n * 256, 256), 256)
            at_up = pl.ds(pl.multiple_of(n * 256 + FF, 256), 256)
            at_down = pl.ds(pl.multiple_of(n * 256 + 2 * FF, 256), 256)

            def low_rank(cols):
                extra = dot_nn(both, q_all[:, cols])
                return extra[:CAP] + extra[CAP:]

            def summed(part, ring, cols):
                return (
                    part[chunk, z, :, cols].astype(F32)
                    + ring[chunk, 0, 3, :, cols].astype(F32)
                    + ring[chunk, 1, 3, :, cols].astype(F32)
                )

            gate_pre = summed(part_gate, ring_gate, at) + low_rank(at)
            up_pre = summed(part_up, ring_up, at) + low_rank(at_up)
            hidden_grad = summed(part_down, ring_down, at) + low_rank(at_down)
            sigmoid = 1.0 / (1.0 + jnp.exp(-gate_pre))
            activated = gate_pre * sigmoid
            slope = sigmoid * (1.0 + gate_pre * (1.0 - sigmoid))
            hidden = (activated * up_pre).astype(BF16)
            gate_grad = (hidden_grad * up_pre * slope).astype(BF16)
            up_grad = (hidden_grad * activated).astype(BF16)
            hidden_own[:, at] = hidden
            place = n * 256 + 512 * (n // 2)
            gathered[chunk, z, :, pl.ds(pl.multiple_of(place, 256), 256)] = gate_grad
            gathered[chunk, z, :, pl.ds(pl.multiple_of(place + 512, 256), 256)] = up_grad
            back = back + dot_nt(gate_grad, q_all[:, at])
            back = back + dot_nt(up_grad, q_all[:, at_up])
            return back + dot_nt(hidden, q_all[:, at_down])

        back = lax.fori_loop(0, 2, tile, jnp.zeros((CAP, 128), F32))
        gather_start(chunk, (0, 1))
        back = lax.fori_loop(2, 4, tile, back)
        lane = lax.broadcasted_iota(jnp.int32, (CAP, 128), 1)
        side = jnp.where(lane < 64, back * scale_row[0:1, :], scaled).astype(BF16)
        gathered[chunk, z, :, pl.ds(2 * FF, 128)] = side
        gather_start(chunk, (2, 3))
        acc_lam[...] += jnp.sum(ranks * back, axis=0, keepdims=True)
        acc_pd[...] += dot_tn(side, hidden_own[...])[96:112]

    def back_rows(rows, n):
        def cols(lo, width):
            return rows[:, :, pl.ds(lo, width)].reshape(n * CAP, width)

        total = dot_nt(cols(0, 512), wg[:, :512]) + dot_nt(cols(512, 512), wu[:, :512])
        total = total + dot_nt(cols(1024, 512), wg[:, 512:]) + dot_nt(cols(1536, 512), wu[:, 512:])
        total = total + dot_nn(cols(2 * FF, 128)[:, :64], p_tok[:64])
        return total.astype(BF16).reshape(n, CAP, D_BLOCK)

    def back_chunk(chunk):
        route_out[chunk] = back_rows(gathered.at[chunk], SHARES)
        send_all(chunk, r_copy, route_out, returned, r_recv)

    opposite = (z + 4) % N_DP

    def back_near(chunk):
        for k in range(SHARES - 1):
            near[k] = gathered[chunk, (z + 5 + k) % N_DP]
        total = back_rows(near, SHARES - 1)
        for k in range(SHARES - 1):
            route_out[chunk, (z + 5 + k) % N_DP] = total[k]
        for j in range(SHARES):
            @pl.when(opposite != j)
            def _():
                r_copy(chunk, j).start()

    def back_far(chunk):
        total = back_rows(gathered.at[chunk, pl.ds(opposite, 1)], 1)
        route_out[chunk, opposite] = total[0]
        for j in range(SHARES):
            @pl.when(opposite == j)
            def _():
                r_copy(chunk, j).start()

    def small_chunk(chunk):
        side = gathered[chunk, :, :, pl.ds(2 * FF, 128)].reshape(ROWS, 128)
        grad_p = dot_tn(side, recv_t[chunk].reshape(ROWS, D_BLOCK))
        gp_ref[0, 0] += grad_p[0:16]
        gp_ref[0, 1] += grad_p[16:32]
        gqd_ref[0] += dot_tn(side, recv_g[chunk].reshape(ROWS, D_BLOCK))[32:48]
        mine = pl.multiple_of(z * 128 + 512 * (z // 4), 128)
        gate_mine = gathered[chunk, :, :, pl.ds(mine, 128)].reshape(ROWS, 128)
        up_mine = gathered[chunk, :, :, pl.ds(pl.multiple_of(mine + 512, 128), 128)].reshape(ROWS, 128)
        gq_ref[0, 0] += dot_tn(side, gate_mine)[64:80]
        gq_ref[0, 1] += dot_tn(side, up_mine)[80:96]

    def combine_chunk(chunk):
        wait_chunk(returned, r_recv, chunk)
        acc_in[...] += dot_tn(hot[chunk], returned[chunk].reshape(ROWS, D_BLOCK))

    p_tok[...] = jnp.zeros_like(p_tok)
    p_grad[...] = jnp.zeros_like(p_grad)
    for base in (0, 64):
        p_tok[base:base + 16, :] = p_in_ref[0, 0]
        p_tok[base + 16:base + 32, :] = p_in_ref[0, 1]
        p_grad[base + 32:base + 48, :] = q_down_ref[0]

    loads[0].wait()
    loads[1].wait()

    @pl.loop(0, CHUNKS)
    def _(chunk):
        route_chunk(chunk)

    pl.semaphore_wait(barrier, N_EXPERT - 1 + N_DP - 1)

    route_send(0)

    q_all[...] = jnp.zeros_like(q_all)
    q_all[0:16, 0:FF] = q_in_ref[0, 0]
    q_all[16:32, FF:2 * FF] = q_in_ref[0, 1]
    q_all[32:48, 2 * FF:] = p_down_ref[0]
    spread = (
        lax.broadcasted_iota(jnp.int32, (RANK, 128), 0) == lax.broadcasted_iota(jnp.int32, (RANK, 128), 1) % 16
    ).astype(F32)
    lanes = lax.broadcasted_iota(jnp.int32, (1, 128), 1)
    wide = jnp.zeros((1, 128), F32)
    for k in range(3):
        scale = lam_ref[k] * mask_ref[k].astype(F32)
        wide = wide + jnp.where((lanes % 64) // 16 == k, dot_nn(scale, spread, HIGH), 0.0)
    scale_row[...] = wide
    acc_in[...] = jnp.zeros_like(acc_in)
    acc_pd[...] = jnp.zeros_like(acc_pd)
    acc_lam[...] = jnp.zeros_like(acc_lam)
    gq_ref[...] = jnp.zeros_like(gq_ref)
    gp_ref[...] = jnp.zeros_like(gp_ref)
    gqd_ref[...] = jnp.zeros_like(gqd_ref)
    loads[2].wait()
    loads[3].wait()
    loads[4].wait()

    def fin_copy(k):
        peer = (z + k) % N_DP
        return pltpu.make_async_remote_copy(
            fin_send.at[peer], fin_recv.at[k], fin_ssem.at[k], fin_rsem.at[k],
            device_id=(peer, e), device_id_type=MESH,
        )

    wait_chunk(recv_t, t_recv, 0)
    route_send(1)
    project(0, recv_t, wg, part_gate)
    ring_start(0, 0)
    forward_up(0)
    ring_start(1, 0)
    forward_down(0)
    ring_start(2, 0)

    @pl.loop(0, CHUNKS + 1)
    def _(i):
        ringing = i < CHUNKS
        gathering = i > 0
        more = i < CHUNKS - 1
        for step in range(1, 4):
            for stream in range(3):
                @pl.when(ringing)
                def _():
                    ring_step(stream, i, step)

                if stream < 2:
                    @pl.when(gathering)
                    def _():
                        gather_step(2 * stream, i - 1, step)
                        gather_step(2 * stream + 1, i - 1, step)

            if step == 1:
                @pl.when(i == CHUNKS)
                def _():
                    for k in range(N_DP):
                        fin_send[k, 0:16, :] = acc_pd[:, k * 128:(k + 1) * 128]
                        fin_send[k, 16:24, :] = jnp.broadcast_to(acc_lam[...], (8, 128))
                    for k in range(1, N_DP):
                        fin_copy(k).start()

                @pl.when(i > 1)
                def _():
                    back_chunk(i - 2)
                    small_chunk(i - 2)

            if step == 2:
                @pl.when(more)
                def _():
                    forward_gate(i + 1)
                    forward_up(i + 1)

                @pl.when(i > 2)
                def _():
                    combine_chunk(i - 3)

            if step == 3:
                @pl.when(i == CHUNKS)
                def _():
                    back_near(CHUNKS - 1)

                @pl.when(more)
                def _():
                    ring_start(0, i + 1)
                    ring_start(1, i + 1)
                    forward_down(i + 1)
                    ring_start(2, i + 1)

                @pl.when(i < CHUNKS - 2)
                def _():
                    route_send(i + 2)

        @pl.when(ringing)
        def _():
            ring_end(i)
            hidden_chunk(i)

        @pl.when(gathering)
        def _():
            gather_end(i - 1)

    back_far(CHUNKS - 1)
    small_chunk(CHUNKS - 1)
    combine_chunk(CHUNKS - 2)
    for k in range(1, N_DP):
        fin_copy(k).wait_recv()
    fin_recv[0] = fin_send[z]
    total = fin_recv[z]
    for k in range(1, N_DP):
        total = total + fin_recv[(z + N_DP - k) % N_DP]
    gpd_ref[0] = total[0:16]
    for k in range(3):
        lam_total = jnp.where(lanes // 16 == k, total[16:17], 0.0)
        gl_ref[k] = dot_nt(lam_total, spread, HIGH) * mask_ref[k].astype(F32)
    combine_chunk(CHUNKS - 1)
    in_grad_ref[...] = acc_in[...].astype(BF16)

    for k in range(1, N_DP):
        fin_copy(k).wait_send()

    @pl.loop(0, CHUNKS)
    def _(chunk):
        for ref, sem in ((send_t, t_send), (send_g, g_send), (route_out, r_send)):
            @pl.when(chunk > 0)
            def _():
                pltpu.make_async_copy(ref.at[chunk], ref.at[chunk], sem.at[chunk]).wait()

            @pl.when(chunk == 0)
            def _():
                sent = ref.at[chunk, pl.ds(1, SHARES - 1)]
                pltpu.make_async_copy(sent, sent, sem.at[chunk]).wait()

    for step in range(4):
        for way in range(2):
            for stream in range(3):
                ring_copy(stream, CHUNKS - 1, way, step).wait_send()
            for half in range(4):
                if way in gather_ways(half, step):
                    gather_copy(half, CHUNKS - 1, way, step).wait_send()


def deliver(*refs):
    for k in range(6):
        refs[k + 6][...] = refs[k][...]


def body(
    tokens, out_grad, routes, route_weights, w_gate, w_up, w_down, p_in, q_in, p_down, q_down, lam, rank_mask
):
    vmem = pl.BlockSpec(memory_space=pltpu.VMEM)
    hbm = pl.BlockSpec(memory_space=pl.ANY)
    dma = pltpu.SemaphoreType.DMA
    grid_rows = (CHUNKS, SHARES, CAP)
    scratch = [
        pltpu.VMEM((TOK, D_BLOCK), BF16),
        pltpu.VMEM((TOK, D_BLOCK), BF16),
        pltpu.VMEM((D_BLOCK, FF), BF16),
        pltpu.VMEM((D_BLOCK, FF), BF16),
        pltpu.VMEM((FF, D_BLOCK), BF16),
        pltpu.VMEM((128, D_BLOCK), BF16),
        pltpu.VMEM((128, D_BLOCK), BF16),
        pltpu.VMEM((128, 3 * FF), BF16),
        pltpu.VMEM((CHUNKS, ROWS, TOK), BF16),
        pltpu.VMEM(grid_rows + (D_BLOCK,), BF16),
        pltpu.VMEM(grid_rows + (D_BLOCK,), BF16),
        pltpu.VMEM(grid_rows + (D_BLOCK,), BF16),
        pltpu.VMEM(grid_rows + (D_BLOCK,), BF16),
        *[pltpu.VMEM(grid_rows + (width,), BF16) for width in WIDTHS],
        *[pltpu.VMEM((CHUNKS, 2, 4, CAP, width), BF16) for width in WIDTHS],
        pltpu.VMEM(grid_rows + (WA,), BF16),
        pltpu.VMEM((SHARES - 1, CAP, WA), BF16),
        pltpu.VMEM(grid_rows + (D_BLOCK,), BF16),
        pltpu.VMEM(grid_rows + (D_BLOCK,), BF16),
        pltpu.VMEM((CAP, FF), BF16),
        pltpu.VMEM((TOK, D_BLOCK), F32),
        pltpu.VMEM((RANK, FF), F32),
        pltpu.VMEM((1, 128), F32),
        pltpu.VMEM((1, 128), F32),
        pltpu.VMEM((2, TOK), F32),
        pltpu.VMEM((N_DP, 24, 128), F32),
        pltpu.VMEM((N_DP, 24, 128), F32),
        dma((5,)),
        dma((CHUNKS,)),
        dma((CHUNKS,)),
        dma((CHUNKS,)),
        dma((CHUNKS,)),
        dma((CHUNKS,)),
        dma((CHUNKS,)),
        dma((3, 2, 4)),
        dma((3, 2, 4)),
        dma((4, 2, 4)),
        dma((4, 2, 4)),
        dma((N_DP,)),
        dma((N_DP,)),
    ]
    results = pl.pallas_call(
        kernel,
        out_shape=(
            jax.ShapeDtypeStruct((TOK, D_BLOCK), BF16),
            jax.ShapeDtypeStruct((1, 2, RANK, FF // N_DP), F32),
            jax.ShapeDtypeStruct((1, 2, RANK, D_BLOCK), F32),
            jax.ShapeDtypeStruct((1, RANK, FF // N_DP), F32),
            jax.ShapeDtypeStruct((1, RANK, D_BLOCK), F32),
            jax.ShapeDtypeStruct((3, 1, RANK), F32),
        ),
        in_specs=[vmem, vmem, hbm, hbm, hbm, hbm, hbm, vmem, vmem, vmem, vmem, vmem, vmem],
        out_specs=(vmem,) * 6,
        scratch_shapes=scratch,
        compiler_params=pltpu.CompilerParams(
            collective_id=0, has_side_effects=True, vmem_limit_bytes=58 * 1024 * 1024
        ),
        name="adapter_backward",
    )(
        routes.T, route_weights.T, tokens, out_grad, w_gate, w_up, w_down, p_in, q_in, p_down, q_down,
        lam.transpose(1, 0, 2), rank_mask.transpose(1, 0, 2),
    )
    results = pl.pallas_call(
        deliver,
        out_shape=tuple(jax.ShapeDtypeStruct(r.shape, r.dtype) for r in results),
        in_specs=[vmem] * 6,
        out_specs=(vmem,) * 6,
        name="deliver",
    )(*results)
    return (*results[:5], results[5].transpose(1, 0, 2))


def solution(mesh):
    in_specs = (
        P("expert", "dp"),
        P("expert", "dp"),
        P("expert", None),
        P("expert", None),
        P("expert", "dp", None),
        P("expert", "dp", None),
        P("expert", None, "dp"),
        P("expert", None, None, "dp"),
        P("expert", None, None, None),
        P("expert", None, None),
        P("expert", None, "dp"),
        P("expert", None, None),
        P("expert", None, None),
    )
    out_specs = (
        P("expert", "dp"),
        P("expert", None, None, "dp"),
        P("expert", None, None, "dp"),
        P("expert", None, "dp"),
        P("expert", None, "dp"),
        P("expert", None, None),
    )
    return jax.shard_map(body, mesh=mesh, in_specs=in_specs, out_specs=out_specs, check_vma=False)
```

```python
import functools

import jax
import jax.numpy as jnp
from jax import lax
from jax.experimental import pallas as pl
from jax.experimental.pallas import tpu as pltpu
from jax.sharding import PartitionSpec as P

MESH = pl.DeviceIdType.MESH
F32 = jnp.float32
BF16 = jnp.bfloat16
HIGH = lax.Precision.HIGHEST

D_BLOCK = 896
FF = 1024
RANK = 16
TOK = 256
CAP = 32
N_DP = 8
N_EXPERT = 32
CHUNKS = 4
SHARES = 8
ROWS = SHARES * CAP
WIDTHS = (FF, FF, FF + 128)
CUTS = (512, 512, 640)
PIECES = (512, 512, 512, 640)
WA = 2 * FF + 128
OFFSETS = (
    ((0, 0), (1, 0), (3, 0), (0, 1)),
    ((1, 1), (3, 3), (3, 1), (1, 3)),
    ((2, 1), (2, 3), (0, 2), (2, 2)),
    ((1, 2), (3, 2), (0, 3), (2, 0)),
)


def dot_nn(a, b, precision=None):
    return lax.dot_general(a, b, (((1,), (0,)), ((), ())), precision=precision, preferred_element_type=F32)


def dot_nt(a, b, precision=None):
    return lax.dot_general(a, b, (((1,), (1,)), ((), ())), precision=precision, preferred_element_type=F32)


def dot_tn(a, b):
    return lax.dot_general(a, b, (((0,), (0,)), ((), ())), preferred_element_type=F32)


def pick(values, chunk):
    if isinstance(chunk, int):
        return values[chunk]
    out = values[0]
    for k in range(1, len(values)):
        out = jnp.where(chunk == k, values[k], out)
    return out


def kernel(
    routes_ref,
    weights_ref,
    tokens_hbm,
    grads_hbm,
    wg_hbm,
    wu_hbm,
    wd_hbm,
    p_in_ref,
    q_in_ref,
    p_down_ref,
    q_down_ref,
    lam_ref,
    mask_ref,
    in_grad_ref,
    gq_ref,
    gp_ref,
    gpd_ref,
    gqd_ref,
    gl_ref,
    tok,
    out_grad,
    wg,
    wu,
    wd,
    p_tok,
    p_grad,
    q_all,
    hot,
    send_t,
    send_g,
    recv_t,
    recv_g,
    part_gate,
    part_up,
    part_down,
    ring_gate,
    ring_up,
    ring_down,
    gathered,
    near,
    route_out,
    returned,
    hidden_own,
    acc_in,
    acc_pd,
    acc_lam,
    scale_row,
    pos,
    fin_send,
    fin_recv,
    load_sem,
    t_send,
    t_recv,
    g_send,
    g_recv,
    r_send,
    r_recv,
    rs_send,
    rs_recv,
    ag_send,
    ag_recv,
    fin_ssem,
    fin_rsem,
):
    z = lax.axis_index("dp")
    e = lax.axis_index("expert")
    ex = e // 8
    ey = (e // 2) % 4
    ec = e % 2
    right = (z + 1) % N_DP
    left = (z + N_DP - 1) % N_DP

    def expert_at(chunk, j, sign):
        dx = pick([o[j // 2][0] for o in OFFSETS], chunk)
        dy = pick([o[j // 2][1] for o in OFFSETS], chunk)
        x = (ex + 4 + sign * dx) % 4
        y = (ey + 4 + sign * dy) % 4
        return (x * 4 + y) * 2 + (ec + j) % 2

    loads = []
    for k, (src, dst) in enumerate(
        (
            (tokens_hbm, tok),
            (grads_hbm, out_grad),
            (wg_hbm.at[0], wg),
            (wu_hbm.at[0], wu),
            (wd_hbm.at[0], wd),
        )
    ):
        copy = pltpu.make_async_copy(src, dst, load_sem.at[k])
        copy.start()
        loads.append(copy)

    barrier = pltpu.get_barrier_semaphore()
    for k in range(1, N_EXPERT):
        pl.semaphore_signal(barrier, inc=1, device_id=(z, (e + k) % N_EXPERT), device_id_type=MESH)
    for k in range(1, N_DP):
        pl.semaphore_signal(barrier, inc=1, device_id=((z + k) % N_DP, e), device_id_type=MESH)

    expert_iota = lax.broadcasted_iota(jnp.int32, (N_EXPERT, TOK), 0)
    named0 = (expert_iota == routes_ref[0:1, :]).astype(F32)
    named1 = (expert_iota == routes_ref[1:2, :]).astype(F32)
    earlier = (
        lax.broadcasted_iota(jnp.int32, (TOK, TOK), 0) < lax.broadcasted_iota(jnp.int32, (TOK, TOK), 1)
    ).astype(BF16)
    before = dot_nn((named0 + named1).astype(BF16), earlier)
    pos[0:1, :] = jnp.sum(named0 * before, axis=0, keepdims=True) + CAP * routes_ref[0:1, :].astype(F32)
    pos[1:2, :] = jnp.sum(named1 * before, axis=0, keepdims=True) + CAP * routes_ref[1:2, :].astype(F32)

    def t_copy(chunk, j):
        return pltpu.make_async_remote_copy(
            send_t.at[chunk, j], recv_t.at[chunk, j], t_send.at[chunk], t_recv.at[chunk],
            device_id=(z, expert_at(chunk, j, -1)), device_id_type=MESH,
        )

    def g_copy(chunk, j):
        return pltpu.make_async_remote_copy(
            send_g.at[chunk, j], recv_g.at[chunk, j], g_send.at[chunk], g_recv.at[chunk],
            device_id=(z, expert_at(chunk, j, -1)), device_id_type=MESH,
        )

    def r_copy(chunk, j):
        return pltpu.make_async_remote_copy(
            route_out.at[chunk, j], returned.at[chunk, j], r_send.at[chunk], r_recv.at[chunk],
            device_id=(z, expert_at(chunk, j, 1)), device_id_type=MESH,
        )

    def send_all(chunk, copy_of, src, dst, sem):
        for j in range(SHARES):
            if j == 0:
                @pl.when(chunk > 0)
                def _():
                    copy_of(chunk, 0).start()

                @pl.when(chunk == 0)
                def _():
                    pltpu.make_async_copy(src.at[chunk, 0], dst.at[chunk, 0], sem.at[chunk]).start()
            else:
                copy_of(chunk, j).start()

    def wait_chunk(ref, sem, chunk):
        pltpu.make_async_copy(ref.at[chunk], ref.at[chunk], sem.at[chunk]).wait()

    slot_iota = lax.broadcasted_iota(jnp.int32, (CAP, TOK), 0)

    def route_chunk(chunk):
        pos0, pos1 = pos[0:1, :], pos[1:2, :]
        weight0, weight1 = weights_ref[0:1, :], weights_ref[1:2, :]
        slot_weights = []
        for j in range(SHARES):
            target = (slot_iota + CAP * expert_at(chunk, j, -1)).astype(F32)
            hit0, hit1 = target == pos0, target == pos1
            hot[chunk, j * CAP:(j + 1) * CAP, :] = jnp.where(hit0 | hit1, 1.0, 0.0).astype(BF16)
            weight = jnp.where(hit0, weight0, 0.0) + jnp.where(hit1, weight1, 0.0)
            slot_weights.append(jnp.sum(weight, axis=1, keepdims=True))
        picked = dot_nn(hot[chunk], tok[...])
        send_t[chunk] = picked.astype(BF16).reshape(SHARES, CAP, D_BLOCK)
        picked = dot_nn(hot[chunk], out_grad[...])
        for j in range(SHARES):
            send_g[chunk, j] = (slot_weights[j] * picked[j * CAP:(j + 1) * CAP, :]).astype(BF16)

    def route_send(chunk):
        send_all(chunk, t_copy, send_t, recv_t, t_recv)
        send_all(chunk, g_copy, send_g, recv_g, g_recv)

    def project(chunk, source, weights, part, transposed=False):
        @pl.loop(0, 2)
        def _(n):
            x = source[chunk].reshape(ROWS, D_BLOCK)
            at = pl.ds(pl.multiple_of(n * 512, 512), 512)
            out = dot_nt(x, weights[at, :]) if transposed else dot_nn(x, weights[:, at])
            part[chunk, :, :, at] = out.astype(BF16).reshape(SHARES, CAP, 512)

    def forward_gate(chunk):
        wait_chunk(recv_t, t_recv, chunk)
        project(chunk, recv_t, wg, part_gate)

    def forward_up(chunk):
        project(chunk, recv_t, wu, part_up)

    def forward_down(chunk):
        wait_chunk(recv_g, g_recv, chunk)
        ranks = dot_nt(recv_t[chunk].reshape(ROWS, D_BLOCK), p_tok[...])
        ranks = ranks + dot_nt(recv_g[chunk].reshape(ROWS, D_BLOCK), p_grad[...])
        part_down[chunk, :, :, pl.ds(FF, 128)] = ranks.astype(BF16).reshape(SHARES, CAP, 128)
        project(chunk, recv_g, wd, part_down, True)

    rings = ((part_gate, ring_gate), (part_up, ring_up), (part_down, ring_down))

    def ring_copy(stream, chunk, way, step):
        part, ring = rings[stream]
        width, cut = WIDTHS[stream], CUTS[stream]
        if step == 0:
            cols = pl.ds(0, cut) if way == 0 else pl.ds(cut, width - cut)
            src = part.at[chunk, (z + 4) % N_DP, :, cols]
            dst = ring.at[chunk, way, 0, :, cols]
        else:
            src, dst = ring.at[chunk, way, step - 1], ring.at[chunk, way, step]
        return pltpu.make_async_remote_copy(
            src, dst, rs_send.at[stream, way, step], rs_recv.at[stream, way, step],
            device_id=(right if way == 0 else left, e), device_id_type=MESH,
        )

    def start_next(copy, chunk):
        if not (isinstance(chunk, int) and chunk == 0):
            @pl.when(chunk > 0)
            def _():
                copy.wait_send()

        copy.start()

    def ring_start(stream, chunk):
        for way in range(2):
            start_next(ring_copy(stream, chunk, way, 0), chunk)

    def ring_step(stream, chunk, step):
        part, ring = rings[stream]
        width, cut = WIDTHS[stream], CUTS[stream]
        for way in range(2):
            ring_copy(stream, chunk, way, step - 1).wait_recv()
            target = (z + 4 - step) % N_DP if way == 0 else (z + 4 + step) % N_DP
            if step == 1:
                lo, hi = (0, cut) if way == 0 else (cut, width)
                total = ring[chunk, way, 0, :, lo:hi].astype(F32) + part[chunk, target, :, lo:hi].astype(F32)
                ring[chunk, way, 0, :, lo:hi] = total.astype(BF16)
                lo, hi = (cut, width) if way == 0 else (0, cut)
                ring[chunk, way, 0, :, lo:hi] = part[chunk, target, :, lo:hi]
            else:
                total = ring[chunk, way, step - 1].astype(F32) + part[chunk, target].astype(F32)
                ring[chunk, way, step - 1] = total.astype(BF16)
            start_next(ring_copy(stream, chunk, way, step), chunk)

    def ring_end(chunk):
        for stream in range(3):
            for way in range(2):
                ring_copy(stream, chunk, way, 3).wait_recv()

    def gather_copy(half, chunk, way, step, arriving=False):
        hops = step + 1 if arriving else step
        owner = (z + N_DP - hops) % N_DP if way == 0 else (z + hops) % N_DP
        ref = gathered.at[chunk, owner, :, pl.ds(half * 512, PIECES[half])]
        return pltpu.make_async_remote_copy(
            ref, ref, ag_send.at[half, way, step], ag_recv.at[half, way, step],
            device_id=(right if way == 0 else left, e), device_id_type=MESH,
        )

    def gather_ways(half, step):
        return (half // 2,) if step == 3 else (0, 1)

    def gather_start(chunk, pieces):
        for half in pieces:
            for way in range(2):
                start_next(gather_copy(half, chunk, way, 0), chunk)

    def gather_step(half, chunk, step):
        for way in range(2):
            gather_copy(half, chunk, way, step - 1, True).wait_recv()
            if way in gather_ways(half, step):
                start_next(gather_copy(half, chunk, way, step), chunk)

    def gather_end(chunk):
        for half in range(4):
            gather_copy(half, chunk, half // 2, 3, True).wait_recv()

    def hidden_chunk(chunk):
        at = pl.ds(FF, 128)
        ranks = (
            part_down[chunk, z, :, at].astype(F32)
            + ring_down[chunk, 0, 3, :, at].astype(F32)
            + ring_down[chunk, 1, 3, :, at].astype(F32)
        )
        scaled = ranks * scale_row[0:1, :]
        high = scaled.astype(BF16)
        low = (scaled - high.astype(F32)).astype(BF16)
        both = jnp.concatenate([high, low], axis=0)

        def tile(n, back):
            at = pl.ds(pl.multiple_of(n * 256, 256), 256)
            at_up = pl.ds(pl.multiple_of(n * 256 + FF, 256), 256)
            at_down = pl.ds(pl.multiple_of(n * 256 + 2 * FF, 256), 256)

            def low_rank(cols):
                extra = dot_nn(both, q_all[:, cols])
                return extra[:CAP] + extra[CAP:]

            def summed(part, ring, cols):
                return (
                    part[chunk, z, :, cols].astype(F32)
                    + ring[chunk, 0, 3, :, cols].astype(F32)
                    + ring[chunk, 1, 3, :, cols].astype(F32)
                )

            gate_pre = summed(part_gate, ring_gate, at) + low_rank(at)
            up_pre = summed(part_up, ring_up, at) + low_rank(at_up)
            hidden_grad = summed(part_down, ring_down, at) + low_rank(at_down)
            sigmoid = 1.0 / (1.0 + jnp.exp(-gate_pre))
            activated = gate_pre * sigmoid
            slope = sigmoid * (1.0 + gate_pre * (1.0 - sigmoid))
            hidden = (activated * up_pre).astype(BF16)
            gate_grad = (hidden_grad * up_pre * slope).astype(BF16)
            up_grad = (hidden_grad * activated).astype(BF16)
            hidden_own[:, at] = hidden
            place = n * 256 + 512 * (n // 2)
            gathered[chunk, z, :, pl.ds(pl.multiple_of(place, 256), 256)] = gate_grad
            gathered[chunk, z, :, pl.ds(pl.multiple_of(place + 512, 256), 256)] = up_grad
            back = back + dot_nt(gate_grad, q_all[:, at])
            back = back + dot_nt(up_grad, q_all[:, at_up])
            return back + dot_nt(hidden, q_all[:, at_down])

        back = lax.fori_loop(0, 2, tile, jnp.zeros((CAP, 128), F32))
        gather_start(chunk, (0, 1))
        back = lax.fori_loop(2, 4, tile, back)
        lane = lax.broadcasted_iota(jnp.int32, (CAP, 128), 1)
        side = jnp.where(lane < 64, back * scale_row[0:1, :], scaled).astype(BF16)
        gathered[chunk, z, :, pl.ds(2 * FF, 128)] = side
        gather_start(chunk, (2, 3))
        acc_lam[...] += jnp.sum(ranks * back, axis=0, keepdims=True)
        acc_pd[...] += dot_tn(side, hidden_own[...])[96:112]

    def back_rows(rows, n):
        def cols(lo, width):
            return rows[:, :, pl.ds(lo, width)].reshape(n * CAP, width)

        total = dot_nt(cols(0, 512), wg[:, :512]) + dot_nt(cols(512, 512), wu[:, :512])
        total = total + dot_nt(cols(1024, 512), wg[:, 512:]) + dot_nt(cols(1536, 512), wu[:, 512:])
        total = total + dot_nn(cols(2 * FF, 128)[:, :64], p_tok[:64])
        return total.astype(BF16).reshape(n, CAP, D_BLOCK)

    def back_chunk(chunk):
        route_out[chunk] = back_rows(gathered.at[chunk], SHARES)
        send_all(chunk, r_copy, route_out, returned, r_recv)

    opposite = (z + 4) % N_DP

    def back_near(chunk):
        for k in range(SHARES - 1):
            near[k] = gathered[chunk, (z + 5 + k) % N_DP]
        total = back_rows(near, SHARES - 1)
        for k in range(SHARES - 1):
            route_out[chunk, (z + 5 + k) % N_DP] = total[k]
        for j in range(SHARES):
            @pl.when(opposite != j)
            def _():
                r_copy(chunk, j).start()

    def back_far(chunk):
        total = back_rows(gathered.at[chunk, pl.ds(opposite, 1)], 1)
        route_out[chunk, opposite] = total[0]
        for j in range(SHARES):
            @pl.when(opposite == j)
            def _():
                r_copy(chunk, j).start()

    def small_chunk(chunk):
        side = gathered[chunk, :, :, pl.ds(2 * FF, 128)].reshape(ROWS, 128)
        grad_p = dot_tn(side, recv_t[chunk].reshape(ROWS, D_BLOCK))
        gp_ref[0, 0] += grad_p[0:16]
        gp_ref[0, 1] += grad_p[16:32]
        gqd_ref[0] += dot_tn(side, recv_g[chunk].reshape(ROWS, D_BLOCK))[32:48]
        mine = pl.multiple_of(z * 128 + 512 * (z // 4), 128)
        gate_mine = gathered[chunk, :, :, pl.ds(mine, 128)].reshape(ROWS, 128)
        up_mine = gathered[chunk, :, :, pl.ds(pl.multiple_of(mine + 512, 128), 128)].reshape(ROWS, 128)
        gq_ref[0, 0] += dot_tn(side, gate_mine)[64:80]
        gq_ref[0, 1] += dot_tn(side, up_mine)[80:96]

    def combine_chunk(chunk):
        wait_chunk(returned, r_recv, chunk)
        acc_in[...] += dot_tn(hot[chunk], returned[chunk].reshape(ROWS, D_BLOCK))

    loads[0].wait()
    loads[1].wait()

    route_chunk(0)
    pl.semaphore_wait(barrier, N_EXPERT - 1 + N_DP - 1)
    route_send(0)

    @pl.loop(1, CHUNKS)
    def _(chunk):
        route_chunk(chunk)

    p_tok[...] = jnp.zeros_like(p_tok)
    p_grad[...] = jnp.zeros_like(p_grad)
    for base in (0, 64):
        p_tok[base:base + 16, :] = p_in_ref[0, 0]
        p_tok[base + 16:base + 32, :] = p_in_ref[0, 1]
        p_grad[base + 32:base + 48, :] = q_down_ref[0]

    q_all[...] = jnp.zeros_like(q_all)
    q_all[0:16, 0:FF] = q_in_ref[0, 0]
    q_all[16:32, FF:2 * FF] = q_in_ref[0, 1]
    q_all[32:48, 2 * FF:] = p_down_ref[0]
    spread = (
        lax.broadcasted_iota(jnp.int32, (RANK, 128), 0) == lax.broadcasted_iota(jnp.int32, (RANK, 128), 1) % 16
    ).astype(F32)
    lanes = lax.broadcasted_iota(jnp.int32, (1, 128), 1)
    wide = jnp.zeros((1, 128), F32)
    for k in range(3):
        scale = lam_ref[k] * mask_ref[k].astype(F32)
        wide = wide + jnp.where((lanes % 64) // 16 == k, dot_nn(scale, spread, HIGH), 0.0)
    scale_row[...] = wide
    acc_in[...] = jnp.zeros_like(acc_in)
    acc_pd[...] = jnp.zeros_like(acc_pd)
    acc_lam[...] = jnp.zeros_like(acc_lam)
    gq_ref[...] = jnp.zeros_like(gq_ref)
    gp_ref[...] = jnp.zeros_like(gp_ref)
    gqd_ref[...] = jnp.zeros_like(gqd_ref)
    loads[2].wait()
    loads[3].wait()
    loads[4].wait()

    def fin_copy(k):
        peer = (z + k) % N_DP
        return pltpu.make_async_remote_copy(
            fin_send.at[peer], fin_recv.at[k], fin_ssem.at[k], fin_rsem.at[k],
            device_id=(peer, e), device_id_type=MESH,
        )

    wait_chunk(recv_t, t_recv, 0)
    project(0, recv_t, wg, part_gate)
    ring_start(0, 0)
    route_send(1)
    forward_up(0)
    ring_start(1, 0)
    forward_down(0)
    ring_start(2, 0)

    @pl.loop(0, CHUNKS + 1)
    def _(i):
        ringing = i < CHUNKS
        gathering = i > 0
        more = i < CHUNKS - 1
        for step in range(1, 4):
            @pl.when(ringing)
            def _():
                for stream in range(3):
                    ring_step(stream, i, step)

            @pl.when(gathering)
            def _():
                for piece in range(4):
                    gather_step(piece, i - 1, step)

            if step == 1:
                @pl.when(i == CHUNKS)
                def _():
                    for k in range(N_DP):
                        fin_send[k, 0:16, :] = acc_pd[:, k * 128:(k + 1) * 128]
                        fin_send[k, 16:24, :] = jnp.broadcast_to(acc_lam[...], (8, 128))
                    for k in range(1, N_DP):
                        fin_copy(k).start()

                @pl.when(i > 1)
                def _():
                    back_chunk(i - 2)
                    small_chunk(i - 2)

            if step == 2:
                @pl.when(more)
                def _():
                    forward_gate(i + 1)
                    forward_up(i + 1)

                @pl.when(i > 2)
                def _():
                    combine_chunk(i - 3)

            if step == 3:
                @pl.when(i == CHUNKS)
                def _():
                    back_near(CHUNKS - 1)

                @pl.when(more)
                def _():
                    ring_start(0, i + 1)
                    ring_start(1, i + 1)
                    forward_down(i + 1)
                    ring_start(2, i + 1)

                @pl.when(i < CHUNKS - 2)
                def _():
                    route_send(i + 2)

        @pl.when(ringing)
        def _():
            ring_end(i)
            hidden_chunk(i)

        @pl.when(gathering)
        def _():
            gather_end(i - 1)

    back_far(CHUNKS - 1)
    small_chunk(CHUNKS - 1)
    combine_chunk(CHUNKS - 2)
    for k in range(1, N_DP):
        fin_copy(k).wait_recv()
    fin_recv[0] = fin_send[z]
    total = fin_recv[z]
    for k in range(1, N_DP):
        total = total + fin_recv[(z + N_DP - k) % N_DP]
    gpd_ref[0] = total[0:16]
    for k in range(3):
        lam_total = jnp.where(lanes // 16 == k, total[16:17], 0.0)
        gl_ref[k] = dot_nt(lam_total, spread, HIGH) * mask_ref[k].astype(F32)
    combine_chunk(CHUNKS - 1)
    in_grad_ref[...] = acc_in[...].astype(BF16)

    for k in range(1, N_DP):
        fin_copy(k).wait_send()

    @pl.loop(0, CHUNKS)
    def _(chunk):
        for ref, sem in ((send_t, t_send), (send_g, g_send), (route_out, r_send)):
            @pl.when(chunk > 0)
            def _():
                pltpu.make_async_copy(ref.at[chunk], ref.at[chunk], sem.at[chunk]).wait()

            @pl.when(chunk == 0)
            def _():
                sent = ref.at[chunk, pl.ds(1, SHARES - 1)]
                pltpu.make_async_copy(sent, sent, sem.at[chunk]).wait()

    for step in range(4):
        for way in range(2):
            for stream in range(3):
                ring_copy(stream, CHUNKS - 1, way, step).wait_send()
            for half in range(4):
                if way in gather_ways(half, step):
                    gather_copy(half, CHUNKS - 1, way, step).wait_send()


def deliver(*refs):
    for k in range(6):
        refs[k + 6][...] = refs[k][...]


def body(
    tokens, out_grad, routes, route_weights, w_gate, w_up, w_down, p_in, q_in, p_down, q_down, lam, rank_mask
):
    vmem = pl.BlockSpec(memory_space=pltpu.VMEM)
    hbm = pl.BlockSpec(memory_space=pl.ANY)
    dma = pltpu.SemaphoreType.DMA
    grid_rows = (CHUNKS, SHARES, CAP)
    scratch = [
        pltpu.VMEM((TOK, D_BLOCK), BF16),
        pltpu.VMEM((TOK, D_BLOCK), BF16),
        pltpu.VMEM((D_BLOCK, FF), BF16),
        pltpu.VMEM((D_BLOCK, FF), BF16),
        pltpu.VMEM((FF, D_BLOCK), BF16),
        pltpu.VMEM((128, D_BLOCK), BF16),
        pltpu.VMEM((128, D_BLOCK), BF16),
        pltpu.VMEM((128, 3 * FF), BF16),
        pltpu.VMEM((CHUNKS, ROWS, TOK), BF16),
        pltpu.VMEM(grid_rows + (D_BLOCK,), BF16),
        pltpu.VMEM(grid_rows + (D_BLOCK,), BF16),
        pltpu.VMEM(grid_rows + (D_BLOCK,), BF16),
        pltpu.VMEM(grid_rows + (D_BLOCK,), BF16),
        *[pltpu.VMEM(grid_rows + (width,), BF16) for width in WIDTHS],
        *[pltpu.VMEM((CHUNKS, 2, 4, CAP, width), BF16) for width in WIDTHS],
        pltpu.VMEM(grid_rows + (WA,), BF16),
        pltpu.VMEM((SHARES - 1, CAP, WA), BF16),
        pltpu.VMEM(grid_rows + (D_BLOCK,), BF16),
        pltpu.VMEM(grid_rows + (D_BLOCK,), BF16),
        pltpu.VMEM((CAP, FF), BF16),
        pltpu.VMEM((TOK, D_BLOCK), F32),
        pltpu.VMEM((RANK, FF), F32),
        pltpu.VMEM((1, 128), F32),
        pltpu.VMEM((1, 128), F32),
        pltpu.VMEM((2, TOK), F32),
        pltpu.VMEM((N_DP, 24, 128), F32),
        pltpu.VMEM((N_DP, 24, 128), F32),
        dma((5,)),
        dma((CHUNKS,)),
        dma((CHUNKS,)),
        dma((CHUNKS,)),
        dma((CHUNKS,)),
        dma((CHUNKS,)),
        dma((CHUNKS,)),
        dma((3, 2, 4)),
        dma((3, 2, 4)),
        dma((4, 2, 4)),
        dma((4, 2, 4)),
        dma((N_DP,)),
        dma((N_DP,)),
    ]
    results = pl.pallas_call(
        kernel,
        out_shape=(
            jax.ShapeDtypeStruct((TOK, D_BLOCK), BF16),
            jax.ShapeDtypeStruct((1, 2, RANK, FF // N_DP), F32),
            jax.ShapeDtypeStruct((1, 2, RANK, D_BLOCK), F32),
            jax.ShapeDtypeStruct((1, RANK, FF // N_DP), F32),
            jax.ShapeDtypeStruct((1, RANK, D_BLOCK), F32),
            jax.ShapeDtypeStruct((3, 1, RANK), F32),
        ),
        in_specs=[vmem, vmem, hbm, hbm, hbm, hbm, hbm, vmem, vmem, vmem, vmem, vmem, vmem],
        out_specs=(vmem,) * 6,
        scratch_shapes=scratch,
        compiler_params=pltpu.CompilerParams(
            collective_id=0, has_side_effects=True, vmem_limit_bytes=58 * 1024 * 1024
        ),
        name="adapter_backward",
    )(
        routes.T, route_weights.T, tokens, out_grad, w_gate, w_up, w_down, p_in, q_in, p_down, q_down,
        lam.transpose(1, 0, 2), rank_mask.transpose(1, 0, 2),
    )
    results = pl.pallas_call(
        deliver,
        out_shape=tuple(jax.ShapeDtypeStruct(r.shape, r.dtype) for r in results),
        in_specs=[vmem] * 6,
        out_specs=(vmem,) * 6,
        name="deliver",
    )(*results)
    return (*results[:5], results[5].transpose(1, 0, 2))


def solution(mesh):
    in_specs = (
        P("expert", "dp"),
        P("expert", "dp"),
        P("expert", None),
        P("expert", None),
        P("expert", "dp", None),
        P("expert", "dp", None),
        P("expert", None, "dp"),
        P("expert", None, None, "dp"),
        P("expert", None, None, None),
        P("expert", None, None),
        P("expert", None, "dp"),
        P("expert", None, None),
        P("expert", None, None),
    )
    out_specs = (
        P("expert", "dp"),
        P("expert", None, None, "dp"),
        P("expert", None, None, "dp"),
        P("expert", None, "dp"),
        P("expert", None, "dp"),
        P("expert", None, None),
    )
    return jax.shard_map(body, mesh=mesh, in_specs=in_specs, out_specs=out_specs, check_vma=False)
```

```python
import functools

import jax
import jax.numpy as jnp
from jax import lax
from jax.experimental import pallas as pl
from jax.experimental.pallas import tpu as pltpu
from jax.sharding import PartitionSpec as P

MESH = pl.DeviceIdType.MESH
F32 = jnp.float32
BF16 = jnp.bfloat16
HIGH = lax.Precision.HIGHEST

D_BLOCK = 896
FF = 1024
RANK = 16
TOK = 256
CAP = 32
N_DP = 8
N_EXPERT = 32
CHUNKS = 4
SHARES = 8
ROWS = SHARES * CAP
WIDTHS = (FF, FF, FF + 128)
CUTS = (512, 512, 640)
PIECES = (512, 512, 512, 640)
WA = 2 * FF + 128
OFFSETS = (
    ((0, 0), (1, 0), (3, 0), (0, 1)),
    ((1, 1), (3, 3), (3, 1), (1, 3)),
    ((2, 1), (2, 3), (0, 2), (2, 2)),
    ((1, 2), (3, 2), (0, 3), (2, 0)),
)


def dot_nn(a, b, precision=None):
    return lax.dot_general(a, b, (((1,), (0,)), ((), ())), precision=precision, preferred_element_type=F32)


def dot_nt(a, b, precision=None):
    return lax.dot_general(a, b, (((1,), (1,)), ((), ())), precision=precision, preferred_element_type=F32)


def dot_tn(a, b):
    return lax.dot_general(a, b, (((0,), (0,)), ((), ())), preferred_element_type=F32)


def pick(values, chunk):
    if isinstance(chunk, int):
        return values[chunk]
    out = values[0]
    for k in range(1, len(values)):
        out = jnp.where(chunk == k, values[k], out)
    return out


def kernel(
    routes_ref,
    weights_ref,
    tokens_hbm,
    grads_hbm,
    wg_hbm,
    wu_hbm,
    wd_hbm,
    p_in_ref,
    q_in_ref,
    p_down_ref,
    q_down_ref,
    lam_ref,
    mask_ref,
    in_grad_ref,
    gq_ref,
    gp_ref,
    gpd_ref,
    gqd_ref,
    gl_ref,
    tok,
    out_grad,
    wg,
    wu,
    wd,
    p_tok,
    p_grad,
    q_all,
    hot,
    send_t,
    send_g,
    recv_t,
    recv_g,
    part_gate,
    part_up,
    part_down,
    ring_gate,
    ring_up,
    ring_down,
    gathered,
    near,
    route_out,
    returned,
    hidden_own,
    acc_in,
    acc_pd,
    acc_lam,
    scale_row,
    pos,
    fin_send,
    fin_recv,
    load_sem,
    t_send,
    t_recv,
    g_send,
    g_recv,
    r_send,
    r_recv,
    rs_send,
    rs_recv,
    ag_send,
    ag_recv,
    fin_ssem,
    fin_rsem,
):
    z = lax.axis_index("dp")
    e = lax.axis_index("expert")
    ex = e // 8
    ey = (e // 2) % 4
    ec = e % 2
    right = (z + 1) % N_DP
    left = (z + N_DP - 1) % N_DP

    def expert_at(chunk, j, sign):
        dx = pick([o[j // 2][0] for o in OFFSETS], chunk)
        dy = pick([o[j // 2][1] for o in OFFSETS], chunk)
        x = (ex + 4 + sign * dx) % 4
        y = (ey + 4 + sign * dy) % 4
        return (x * 4 + y) * 2 + (ec + j) % 2

    loads = []
    for k, (src, dst) in enumerate(
        (
            (tokens_hbm, tok),
            (grads_hbm, out_grad),
            (wg_hbm.at[0], wg),
            (wu_hbm.at[0], wu),
            (wd_hbm.at[0], wd),
        )
    ):
        copy = pltpu.make_async_copy(src, dst, load_sem.at[k])
        copy.start()
        loads.append(copy)

    barrier = pltpu.get_barrier_semaphore()
    for k in range(1, N_EXPERT):
        pl.semaphore_signal(barrier, inc=1, device_id=(z, (e + k) % N_EXPERT), device_id_type=MESH)
    for k in range(1, N_DP):
        pl.semaphore_signal(barrier, inc=1, device_id=((z + k) % N_DP, e), device_id_type=MESH)

    expert_iota = lax.broadcasted_iota(jnp.int32, (N_EXPERT, TOK), 0)
    named0 = (expert_iota == routes_ref[0:1, :]).astype(F32)
    named1 = (expert_iota == routes_ref[1:2, :]).astype(F32)
    earlier = (
        lax.broadcasted_iota(jnp.int32, (TOK, TOK), 0) < lax.broadcasted_iota(jnp.int32, (TOK, TOK), 1)
    ).astype(BF16)
    before = dot_nn((named0 + named1).astype(BF16), earlier)
    pos[0:1, :] = jnp.sum(named0 * before, axis=0, keepdims=True) + CAP * routes_ref[0:1, :].astype(F32)
    pos[1:2, :] = jnp.sum(named1 * before, axis=0, keepdims=True) + CAP * routes_ref[1:2, :].astype(F32)

    def t_copy(chunk, j):
        return pltpu.make_async_remote_copy(
            send_t.at[chunk, j], recv_t.at[chunk, j], t_send.at[chunk], t_recv.at[chunk],
            device_id=(z, expert_at(chunk, j, -1)), device_id_type=MESH,
        )

    def g_copy(chunk, j):
        return pltpu.make_async_remote_copy(
            send_g.at[chunk, j], recv_g.at[chunk, j], g_send.at[chunk], g_recv.at[chunk],
            device_id=(z, expert_at(chunk, j, -1)), device_id_type=MESH,
        )

    def r_copy(chunk, j):
        return pltpu.make_async_remote_copy(
            route_out.at[chunk, j], returned.at[chunk, j], r_send.at[chunk], r_recv.at[chunk],
            device_id=(z, expert_at(chunk, j, 1)), device_id_type=MESH,
        )

    def send_all(chunk, copy_of, src, dst, sem):
        for j in range(SHARES):
            if j == 0:
                @pl.when(chunk > 0)
                def _():
                    copy_of(chunk, 0).start()

                @pl.when(chunk == 0)
                def _():
                    pltpu.make_async_copy(src.at[chunk, 0], dst.at[chunk, 0], sem.at[chunk]).start()
            else:
                copy_of(chunk, j).start()

    def wait_chunk(ref, sem, chunk):
        pltpu.make_async_copy(ref.at[chunk], ref.at[chunk], sem.at[chunk]).wait()

    slot_iota = lax.broadcasted_iota(jnp.int32, (CAP, TOK), 0)

    def route_chunk(chunk):
        pos0, pos1 = pos[0:1, :], pos[1:2, :]
        weight0, weight1 = weights_ref[0:1, :], weights_ref[1:2, :]
        slot_weights = []
        for j in range(SHARES):
            target = (slot_iota + CAP * expert_at(chunk, j, -1)).astype(F32)
            hit0, hit1 = target == pos0, target == pos1
            hot[chunk, j * CAP:(j + 1) * CAP, :] = jnp.where(hit0 | hit1, 1.0, 0.0).astype(BF16)
            weight = jnp.where(hit0, weight0, 0.0) + jnp.where(hit1, weight1, 0.0)
            slot_weights.append(jnp.sum(weight, axis=1, keepdims=True))
        picked = dot_nn(hot[chunk], tok[...])
        send_t[chunk] = picked.astype(BF16).reshape(SHARES, CAP, D_BLOCK)
        picked = dot_nn(hot[chunk], out_grad[...])
        for j in range(SHARES):
            send_g[chunk, j] = (slot_weights[j] * picked[j * CAP:(j + 1) * CAP, :]).astype(BF16)

    def route_send(chunk):
        send_all(chunk, t_copy, send_t, recv_t, t_recv)
        send_all(chunk, g_copy, send_g, recv_g, g_recv)

    def project(chunk, source, weights, part, transposed=False):
        @pl.loop(0, 2)
        def _(n):
            x = source[chunk].reshape(ROWS, D_BLOCK)
            at = pl.ds(pl.multiple_of(n * 512, 512), 512)
            out = dot_nt(x, weights[at, :]) if transposed else dot_nn(x, weights[:, at])
            part[chunk, :, :, at] = out.astype(BF16).reshape(SHARES, CAP, 512)

    def forward_gate(chunk):
        wait_chunk(recv_t, t_recv, chunk)
        project(chunk, recv_t, wg, part_gate)

    def forward_up(chunk):
        project(chunk, recv_t, wu, part_up)

    def forward_down(chunk):
        wait_chunk(recv_g, g_recv, chunk)
        ranks = dot_nt(recv_t[chunk].reshape(ROWS, D_BLOCK), p_tok[...])
        ranks = ranks + dot_nt(recv_g[chunk].reshape(ROWS, D_BLOCK), p_grad[...])
        part_down[chunk, :, :, pl.ds(FF, 128)] = ranks.astype(BF16).reshape(SHARES, CAP, 128)
        project(chunk, recv_g, wd, part_down, True)

    rings = ((part_gate, ring_gate), (part_up, ring_up), (part_down, ring_down))

    def ring_copy(stream, chunk, way, step):
        part, ring = rings[stream]
        width, cut = WIDTHS[stream], CUTS[stream]
        if step == 0:
            cols = pl.ds(0, cut) if way == 0 else pl.ds(cut, width - cut)
            src = part.at[chunk, (z + 4) % N_DP, :, cols]
            dst = ring.at[chunk, way, 0, :, cols]
        else:
            src, dst = ring.at[chunk, way, step - 1], ring.at[chunk, way, step]
        return pltpu.make_async_remote_copy(
            src, dst, rs_send.at[stream, way, step], rs_recv.at[stream, way, step],
            device_id=(right if way == 0 else left, e), device_id_type=MESH,
        )

    def start_next(copy, chunk):
        if not (isinstance(chunk, int) and chunk == 0):
            @pl.when(chunk > 0)
            def _():
                copy.wait_send()

        copy.start()

    def ring_start(stream, chunk):
        for way in range(2):
            start_next(ring_copy(stream, chunk, way, 0), chunk)

    def ring_step(stream, chunk, step):
        part, ring = rings[stream]
        width, cut = WIDTHS[stream], CUTS[stream]
        for way in range(2):
            ring_copy(stream, chunk, way, step - 1).wait_recv()
            target = (z + 4 - step) % N_DP if way == 0 else (z + 4 + step) % N_DP
            if step == 1:
                lo, hi = (0, cut) if way == 0 else (cut, width)
                total = ring[chunk, way, 0, :, lo:hi].astype(F32) + part[chunk, target, :, lo:hi].astype(F32)
                ring[chunk, way, 0, :, lo:hi] = total.astype(BF16)
                lo, hi = (cut, width) if way == 0 else (0, cut)
                ring[chunk, way, 0, :, lo:hi] = part[chunk, target, :, lo:hi]
            else:
                total = ring[chunk, way, step - 1].astype(F32) + part[chunk, target].astype(F32)
                ring[chunk, way, step - 1] = total.astype(BF16)
            start_next(ring_copy(stream, chunk, way, step), chunk)

    def ring_end(chunk):
        for stream in range(3):
            for way in range(2):
                ring_copy(stream, chunk, way, 3).wait_recv()

    def gather_copy(half, chunk, way, step, arriving=False):
        hops = step + 1 if arriving else step
        owner = (z + N_DP - hops) % N_DP if way == 0 else (z + hops) % N_DP
        ref = gathered.at[chunk, owner, :, pl.ds(half * 512, PIECES[half])]
        return pltpu.make_async_remote_copy(
            ref, ref, ag_send.at[half, way, step], ag_recv.at[half, way, step],
            device_id=(right if way == 0 else left, e), device_id_type=MESH,
        )

    def gather_ways(half, step):
        return (half // 2,) if step == 3 else (0, 1)

    def gather_start(chunk, pieces):
        for half in pieces:
            for way in range(2):
                start_next(gather_copy(half, chunk, way, 0), chunk)

    def gather_step(half, chunk, step):
        for way in range(2):
            gather_copy(half, chunk, way, step - 1, True).wait_recv()
            if way in gather_ways(half, step):
                start_next(gather_copy(half, chunk, way, step), chunk)

    def gather_end(chunk):
        for half in range(4):
            gather_copy(half, chunk, half // 2, 3, True).wait_recv()

    def hidden_chunk(chunk):
        at = pl.ds(FF, 128)
        ranks = (
            part_down[chunk, z, :, at].astype(F32)
            + ring_down[chunk, 0, 3, :, at].astype(F32)
            + ring_down[chunk, 1, 3, :, at].astype(F32)
        )
        scaled = ranks * scale_row[0:1, :]
        high = scaled.astype(BF16)
        low = (scaled - high.astype(F32)).astype(BF16)
        both = jnp.concatenate([high, low], axis=0)

        def tile(n, back):
            at = pl.ds(pl.multiple_of(n * 256, 256), 256)
            at_up = pl.ds(pl.multiple_of(n * 256 + FF, 256), 256)
            at_down = pl.ds(pl.multiple_of(n * 256 + 2 * FF, 256), 256)

            def low_rank(cols):
                extra = dot_nn(both, q_all[:, cols])
                return extra[:CAP] + extra[CAP:]

            def summed(part, ring, cols):
                return (
                    part[chunk, z, :, cols].astype(F32)
                    + ring[chunk, 0, 3, :, cols].astype(F32)
                    + ring[chunk, 1, 3, :, cols].astype(F32)
                )

            gate_pre = summed(part_gate, ring_gate, at) + low_rank(at)
            up_pre = summed(part_up, ring_up, at) + low_rank(at_up)
            hidden_grad = summed(part_down, ring_down, at) + low_rank(at_down)
            sigmoid = 1.0 / (1.0 + jnp.exp(-gate_pre))
            activated = gate_pre * sigmoid
            slope = sigmoid * (1.0 + gate_pre * (1.0 - sigmoid))
            hidden = (activated * up_pre).astype(BF16)
            gate_grad = (hidden_grad * up_pre * slope).astype(BF16)
            up_grad = (hidden_grad * activated).astype(BF16)
            hidden_own[:, at] = hidden
            place = n * 256 + 512 * (n // 2)
            gathered[chunk, z, :, pl.ds(pl.multiple_of(place, 256), 256)] = gate_grad
            gathered[chunk, z, :, pl.ds(pl.multiple_of(place + 512, 256), 256)] = up_grad
            back = back + dot_nt(gate_grad, q_all[:, at])
            back = back + dot_nt(up_grad, q_all[:, at_up])
            return back + dot_nt(hidden, q_all[:, at_down])

        back = lax.fori_loop(0, 2, tile, jnp.zeros((CAP, 128), F32))
        gather_start(chunk, (0, 1))
        back = lax.fori_loop(2, 4, tile, back)
        lane = lax.broadcasted_iota(jnp.int32, (CAP, 128), 1)
        side = jnp.where(lane < 64, back * scale_row[0:1, :], scaled).astype(BF16)
        gathered[chunk, z, :, pl.ds(2 * FF, 128)] = side
        gather_start(chunk, (2, 3))
        acc_lam[...] += jnp.sum(ranks * back, axis=0, keepdims=True)
        acc_pd[...] += dot_tn(side, hidden_own[...])[96:112]

    def back_rows(rows, n):
        def cols(lo, width):
            return rows[:, :, pl.ds(lo, width)].reshape(n * CAP, width)

        total = dot_nt(cols(0, 512), wg[:, :512]) + dot_nt(cols(512, 512), wu[:, :512])
        total = total + dot_nt(cols(1024, 512), wg[:, 512:]) + dot_nt(cols(1536, 512), wu[:, 512:])
        total = total + dot_nn(cols(2 * FF, 128)[:, :64], p_tok[:64])
        return total.astype(BF16).reshape(n, CAP, D_BLOCK)

    def back_chunk(chunk):
        route_out[chunk] = back_rows(gathered.at[chunk], SHARES)
        send_all(chunk, r_copy, route_out, returned, r_recv)

    opposite = (z + 4) % N_DP

    def back_near(chunk):
        for k in range(SHARES - 1):
            near[k] = gathered[chunk, (z + 5 + k) % N_DP]
        total = back_rows(near, SHARES - 1)
        for k in range(SHARES - 1):
            route_out[chunk, (z + 5 + k) % N_DP] = total[k]
        for j in range(SHARES):
            @pl.when(opposite != j)
            def _():
                r_copy(chunk, j).start()

    def back_far(chunk):
        total = back_rows(gathered.at[chunk, pl.ds(opposite, 1)], 1)
        route_out[chunk, opposite] = total[0]
        for j in range(SHARES):
            @pl.when(opposite == j)
            def _():
                r_copy(chunk, j).start()

    def small_chunk(chunk):
        side = gathered[chunk, :, :, pl.ds(2 * FF, 128)].reshape(ROWS, 128)
        grad_p = dot_tn(side, recv_t[chunk].reshape(ROWS, D_BLOCK))
        gp_ref[0, 0] += grad_p[0:16]
        gp_ref[0, 1] += grad_p[16:32]
        gqd_ref[0] += dot_tn(side, recv_g[chunk].reshape(ROWS, D_BLOCK))[32:48]
        mine = pl.multiple_of(z * 128 + 512 * (z // 4), 128)
        gate_mine = gathered[chunk, :, :, pl.ds(mine, 128)].reshape(ROWS, 128)
        up_mine = gathered[chunk, :, :, pl.ds(pl.multiple_of(mine + 512, 128), 128)].reshape(ROWS, 128)
        gq_ref[0, 0] += dot_tn(side, gate_mine)[64:80]
        gq_ref[0, 1] += dot_tn(side, up_mine)[80:96]

    def combine_chunk(chunk):
        wait_chunk(returned, r_recv, chunk)
        acc_in[...] += dot_tn(hot[chunk], returned[chunk].reshape(ROWS, D_BLOCK))

    loads[0].wait()
    loads[1].wait()

    route_chunk(0)
    pl.semaphore_wait(barrier, N_EXPERT - 1 + N_DP - 1)
    route_send(0)

    @pl.loop(1, CHUNKS)
    def _(chunk):
        route_chunk(chunk)

    p_tok[...] = jnp.zeros_like(p_tok)
    p_grad[...] = jnp.zeros_like(p_grad)
    for base in (0, 64):
        p_tok[base:base + 16, :] = p_in_ref[0, 0]
        p_tok[base + 16:base + 32, :] = p_in_ref[0, 1]
        p_grad[base + 32:base + 48, :] = q_down_ref[0]

    q_all[...] = jnp.zeros_like(q_all)
    q_all[0:16, 0:FF] = q_in_ref[0, 0]
    q_all[16:32, FF:2 * FF] = q_in_ref[0, 1]
    q_all[32:48, 2 * FF:] = p_down_ref[0]
    spread = (
        lax.broadcasted_iota(jnp.int32, (RANK, 128), 0) == lax.broadcasted_iota(jnp.int32, (RANK, 128), 1) % 16
    ).astype(F32)
    lanes = lax.broadcasted_iota(jnp.int32, (1, 128), 1)
    wide = jnp.zeros((1, 128), F32)
    for k in range(3):
        scale = lam_ref[k] * mask_ref[k].astype(F32)
        wide = wide + jnp.where((lanes % 64) // 16 == k, dot_nn(scale, spread, HIGH), 0.0)
    scale_row[...] = wide
    acc_in[...] = jnp.zeros_like(acc_in)
    acc_pd[...] = jnp.zeros_like(acc_pd)
    acc_lam[...] = jnp.zeros_like(acc_lam)
    gq_ref[...] = jnp.zeros_like(gq_ref)
    gp_ref[...] = jnp.zeros_like(gp_ref)
    gqd_ref[...] = jnp.zeros_like(gqd_ref)
    loads[2].wait()
    loads[3].wait()
    loads[4].wait()

    def fin_copy(k):
        peer = (z + k) % N_DP
        return pltpu.make_async_remote_copy(
            fin_send.at[peer], fin_recv.at[k], fin_ssem.at[k], fin_rsem.at[k],
            device_id=(peer, e), device_id_type=MESH,
        )

    wait_chunk(recv_t, t_recv, 0)
    project(0, recv_t, wg, part_gate)
    ring_start(0, 0)
    route_send(1)
    forward_up(0)
    ring_start(1, 0)
    forward_down(0)
    ring_start(2, 0)

    @pl.loop(0, CHUNKS + 1)
    def _(i):
        ringing = i < CHUNKS
        gathering = i > 0
        more = i < CHUNKS - 1
        for step in range(1, 4):
            @pl.when(ringing)
            def _():
                for stream in range(3):
                    ring_step(stream, i, step)

            @pl.when(gathering)
            def _():
                for piece in range(4):
                    gather_step(piece, i - 1, step)

            if step == 1:
                @pl.when(i > 1)
                def _():
                    back_chunk(i - 2)
                    small_chunk(i - 2)

            if step == 2:
                @pl.when(more)
                def _():
                    forward_gate(i + 1)
                    forward_up(i + 1)

                @pl.when(i > 2)
                def _():
                    combine_chunk(i - 3)

            if step == 3:
                @pl.when(i == CHUNKS)
                def _():
                    for k in range(N_DP):
                        fin_send[k, 0:16, :] = acc_pd[:, k * 128:(k + 1) * 128]
                        fin_send[k, 16:24, :] = jnp.broadcast_to(acc_lam[...], (8, 128))
                    for k in range(1, N_DP):
                        fin_copy(k).start()

                @pl.when(i == CHUNKS)
                def _():
                    back_near(CHUNKS - 1)

                @pl.when(more)
                def _():
                    ring_start(0, i + 1)
                    ring_start(1, i + 1)
                    forward_down(i + 1)
                    ring_start(2, i + 1)

                @pl.when(i < CHUNKS - 2)
                def _():
                    route_send(i + 2)

        @pl.when(ringing)
        def _():
            ring_end(i)
            hidden_chunk(i)

        @pl.when(gathering)
        def _():
            gather_end(i - 1)

    back_far(CHUNKS - 1)
    small_chunk(CHUNKS - 1)
    combine_chunk(CHUNKS - 2)
    for k in range(1, N_DP):
        fin_copy(k).wait_recv()
    fin_recv[0] = fin_send[z]
    total = fin_recv[z]
    for k in range(1, N_DP):
        total = total + fin_recv[(z + N_DP - k) % N_DP]
    gpd_ref[0] = total[0:16]
    for k in range(3):
        lam_total = jnp.where(lanes // 16 == k, total[16:17], 0.0)
        gl_ref[k] = dot_nt(lam_total, spread, HIGH) * mask_ref[k].astype(F32)
    combine_chunk(CHUNKS - 1)
    in_grad_ref[...] = acc_in[...].astype(BF16)

    for k in range(1, N_DP):
        fin_copy(k).wait_send()

    @pl.loop(0, CHUNKS)
    def _(chunk):
        for ref, sem in ((send_t, t_send), (send_g, g_send), (route_out, r_send)):
            @pl.when(chunk > 0)
            def _():
                pltpu.make_async_copy(ref.at[chunk], ref.at[chunk], sem.at[chunk]).wait()

            @pl.when(chunk == 0)
            def _():
                sent = ref.at[chunk, pl.ds(1, SHARES - 1)]
                pltpu.make_async_copy(sent, sent, sem.at[chunk]).wait()

    for step in range(4):
        for way in range(2):
            for stream in range(3):
                ring_copy(stream, CHUNKS - 1, way, step).wait_send()
            for half in range(4):
                if way in gather_ways(half, step):
                    gather_copy(half, CHUNKS - 1, way, step).wait_send()


def deliver(*refs):
    for k in range(6):
        refs[k + 6][...] = refs[k][...]


def body(
    tokens, out_grad, routes, route_weights, w_gate, w_up, w_down, p_in, q_in, p_down, q_down, lam, rank_mask
):
    vmem = pl.BlockSpec(memory_space=pltpu.VMEM)
    hbm = pl.BlockSpec(memory_space=pl.ANY)
    dma = pltpu.SemaphoreType.DMA
    grid_rows = (CHUNKS, SHARES, CAP)
    scratch = [
        pltpu.VMEM((TOK, D_BLOCK), BF16),
        pltpu.VMEM((TOK, D_BLOCK), BF16),
        pltpu.VMEM((D_BLOCK, FF), BF16),
        pltpu.VMEM((D_BLOCK, FF), BF16),
        pltpu.VMEM((FF, D_BLOCK), BF16),
        pltpu.VMEM((128, D_BLOCK), BF16),
        pltpu.VMEM((128, D_BLOCK), BF16),
        pltpu.VMEM((128, 3 * FF), BF16),
        pltpu.VMEM((CHUNKS, ROWS, TOK), BF16),
        pltpu.VMEM(grid_rows + (D_BLOCK,), BF16),
        pltpu.VMEM(grid_rows + (D_BLOCK,), BF16),
        pltpu.VMEM(grid_rows + (D_BLOCK,), BF16),
        pltpu.VMEM(grid_rows + (D_BLOCK,), BF16),
        *[pltpu.VMEM(grid_rows + (width,), BF16) for width in WIDTHS],
        *[pltpu.VMEM((CHUNKS, 2, 4, CAP, width), BF16) for width in WIDTHS],
        pltpu.VMEM(grid_rows + (WA,), BF16),
        pltpu.VMEM((SHARES - 1, CAP, WA), BF16),
        pltpu.VMEM(grid_rows + (D_BLOCK,), BF16),
        pltpu.VMEM(grid_rows + (D_BLOCK,), BF16),
        pltpu.VMEM((CAP, FF), BF16),
        pltpu.VMEM((TOK, D_BLOCK), F32),
        pltpu.VMEM((RANK, FF), F32),
        pltpu.VMEM((1, 128), F32),
        pltpu.VMEM((1, 128), F32),
        pltpu.VMEM((2, TOK), F32),
        pltpu.VMEM((N_DP, 24, 128), F32),
        pltpu.VMEM((N_DP, 24, 128), F32),
        dma((5,)),
        dma((CHUNKS,)),
        dma((CHUNKS,)),
        dma((CHUNKS,)),
        dma((CHUNKS,)),
        dma((CHUNKS,)),
        dma((CHUNKS,)),
        dma((3, 2, 4)),
        dma((3, 2, 4)),
        dma((4, 2, 4)),
        dma((4, 2, 4)),
        dma((N_DP,)),
        dma((N_DP,)),
    ]
    results = pl.pallas_call(
        kernel,
        out_shape=(
            jax.ShapeDtypeStruct((TOK, D_BLOCK), BF16),
            jax.ShapeDtypeStruct((1, 2, RANK, FF // N_DP), F32),
            jax.ShapeDtypeStruct((1, 2, RANK, D_BLOCK), F32),
            jax.ShapeDtypeStruct((1, RANK, FF // N_DP), F32),
            jax.ShapeDtypeStruct((1, RANK, D_BLOCK), F32),
            jax.ShapeDtypeStruct((3, 1, RANK), F32),
        ),
        in_specs=[vmem, vmem, hbm, hbm, hbm, hbm, hbm, vmem, vmem, vmem, vmem, vmem, vmem],
        out_specs=(vmem,) * 6,
        scratch_shapes=scratch,
        compiler_params=pltpu.CompilerParams(
            collective_id=0, has_side_effects=True, vmem_limit_bytes=58 * 1024 * 1024
        ),
        name="adapter_backward",
    )(
        routes.T, route_weights.T, tokens, out_grad, w_gate, w_up, w_down, p_in, q_in, p_down, q_down,
        lam.transpose(1, 0, 2), rank_mask.transpose(1, 0, 2),
    )
    results = pl.pallas_call(
        deliver,
        out_shape=tuple(jax.ShapeDtypeStruct(r.shape, r.dtype) for r in results),
        in_specs=[vmem] * 6,
        out_specs=(vmem,) * 6,
        name="deliver",
    )(*results)
    return (*results[:5], results[5].transpose(1, 0, 2))


def solution(mesh):
    in_specs = (
        P("expert", "dp"),
        P("expert", "dp"),
        P("expert", None),
        P("expert", None),
        P("expert", "dp", None),
        P("expert", "dp", None),
        P("expert", None, "dp"),
        P("expert", None, None, "dp"),
        P("expert", None, None, None),
        P("expert", None, None),
        P("expert", None, "dp"),
        P("expert", None, None),
        P("expert", None, None),
    )
    out_specs = (
        P("expert", "dp"),
        P("expert", None, None, "dp"),
        P("expert", None, None, "dp"),
        P("expert", None, "dp"),
        P("expert", None, "dp"),
        P("expert", None, None),
    )
    return jax.shard_map(body, mesh=mesh, in_specs=in_specs, out_specs=out_specs, check_vma=False)
```
